128 devices in a mesh: gx: 8 (over y, x_hi), gy: 4 (over z), ta: 4 (over x_lo, core).
Axes of the slice: x: 4 (x_hi: 2, x_lo: 2; x = x_hi * 2 + x_lo), y: 4, z: 4, core: 2. Of those that a mesh axis runs over, the one named last changes fastest.
Arguments:
- field: float32 [1024, 1024, 512], P('gx', 'gy', 'ta'), may hold values from -32 to 32
- init_y: float32 [1024, 64], P('gy'), may hold values from -0.1875 to 0.1875
- init_t: float32 [512, 32], P('ta'), may hold values from -0.25 to 0.25
- sketch_x: float32 [2048, 64], replicated, may hold values from -0.125 to 0.125
- sketch_y: float32 [2048, 64], replicated, may hold values from -0.125 to 0.125
- sketch_t: float32 [4096, 32], replicated, may hold values from -0.09375 to 0.09375
Outputs:
- factor_x: float32 [1024, 64], P('gx')
- factor_y: float32 [1024, 64], P('gy')
- factor_t: float32 [512, 32], P('ta')
- core: float32 [64, 2048], replicated
The draws below stay inside these ranges and needn't reach their ends.
All inputs are finite; a program needn't handle non-finite values.
Results may differ from the reference program's by a relative error of at most 0.00024.
Values sent between devices are 32-bit elements; how exact they have to be, the bound alone decides.
No kernel may reach another device: no remote copies, remote signals or barrier semaphores. Data moves between devices by JAX's collectives and lax.ppermute only.
A program may use at most 128 MiB of HBM per device.

```python
import math
import jax
import jax.numpy as jnp
from jax import lax

R1 = 64
R2 = 64
R3 = 32
NX = 1024
NY = 1024
NT = 512


def draw_field(key, part):
    key = jax.random.fold_in(key, 7)
    key_x, key_y, key_t, key_n = jax.random.split(key, 4)
    low = math.log(0.5)
    high = math.log(2.0)
    scale_x = jnp.exp(jax.random.uniform(key_x, (NX, 1, 1), jnp.float32, low, high))
    scale_y = jnp.exp(jax.random.uniform(key_y, (1, NY, 1), jnp.float32, low, high))
    scale_t = jnp.exp(jax.random.uniform(key_t, (1, 1, NT), jnp.float32, low, high))
    noise = jax.random.truncated_normal(key_n, -4.0, 4.0, (NX, NY, NT), jnp.float32)
    return (noise * scale_x * scale_y * scale_t).astype(jnp.float32)


def block_scale(rng, dims, cuts, low, top_value):
    level, own = 1.0, jax.random.fold_in(rng, 6)
    for dim, blocks in cuts:
        heights = jnp.exp(jax.random.uniform(jax.random.fold_in(own, dim), (blocks,), jnp.float32, low / len(cuts), top_value / len(cuts)))
        level = level * jnp.repeat(heights, dims[dim] // blocks).reshape([-1 if axis == dim else 1 for axis in range(len(dims))])
    return level


def scatter_about(own_key, dims, deviation, bound, pieces=(), dtype=jnp.bfloat16):
    values = jax.random.normal(own_key, dims, jnp.float32) * deviation
    if len(pieces) > 0:
        values = block_scale(own_key, dims, pieces, -0.22, 0.18) * values
    return jnp.clip(values, min=-bound, max=bound).astype(dtype)


def setup_inputs(seed: int = 0) -> dict:
    arg_keys = jax.random.split(jax.random.key(seed), 7)
    return {
        "field": draw_field(jax.random.fold_in(arg_keys[6], 71), 0),
        "init_y": scatter_about(arg_keys[1], (NY, R2), NY ** -0.5, 0.1875, ((0, 4),), jnp.float32),
        "init_t": scatter_about(arg_keys[2], (NT, R3), NT ** -0.5, 0.25, ((0, 4),), jnp.float32),
        "sketch_x": scatter_about(arg_keys[3], (R2 * R3, R1), (R2 * R3) ** -0.5, 0.125, (), jnp.float32),
        "sketch_y": scatter_about(arg_keys[4], (R1 * R3, R2), (R1 * R3) ** -0.5, 0.125, (), jnp.float32),
        "sketch_t": scatter_about(arg_keys[5], (R1 * R2, R3), (R1 * R2) ** -0.5, 0.09375, (), jnp.float32),
    }


HIGH = lax.Precision.HIGHEST

def orthonormal(zmat):
    gram = jnp.dot(zmat.T, zmat, precision=HIGH)
    lower = jnp.linalg.cholesky(gram)
    return jax.scipy.linalg.solve_triangular(lower, zmat.T, lower=True).T

def reference(field, init_y, init_t, sketch_x, sketch_y, sketch_t):
    w_time = jnp.einsum('xyt,tc->xyc', field, init_t, precision=HIGH)
    unfold_x = jnp.einsum('xyc,ya->xac', w_time, init_y, precision=HIGH).reshape(NX, R2 * R3)
    q_x = orthonormal(jnp.dot(unfold_x, sketch_x, precision=HIGH))
    unfold_y = jnp.einsum('xyc,xb->ybc', w_time, q_x, precision=HIGH).reshape(NY, R1 * R3)
    q_y = orthonormal(jnp.dot(unfold_y, sketch_y, precision=HIGH))
    w_xdir = jnp.einsum('xyt,xb->byt', field, q_x, precision=HIGH)
    unfold_t = jnp.einsum('byt,ya->tba', w_xdir, q_y, precision=HIGH)
    q_t = orthonormal(jnp.dot(unfold_t.reshape(NT, R1 * R2), sketch_t, precision=HIGH))
    core = jnp.einsum('tba,tc->bac', unfold_t, q_t, precision=HIGH).reshape(R1, R2 * R3)
    return (q_x * math.sqrt(NX), q_y * math.sqrt(NY), q_t * math.sqrt(NT), core)
```

```python
import math

import jax
import jax.numpy as jnp
from jax import lax
from jax.sharding import Mesh, PartitionSpec as P

HIGH = lax.Precision.HIGHEST
MID = lax.Precision.HIGH


def pair(x):
    return lax.ppermute(x, "c", [(0, 1), (1, 0)])


def spread(x, axes):
    n = math.prod(lax.axis_size(a) for a in axes)
    return lax.all_to_all(jnp.broadcast_to(x, (n,) + x.shape), axes, 0, 0)


def total(x, axes):
    return spread(x, axes).sum(0)


def half_sum(x):
    n = x.shape[0] // 2
    me = lax.axis_index("c")
    mine = lax.dynamic_slice_in_dim(x, me * n, n, 0)
    other = lax.dynamic_slice_in_dim(x, (1 - me) * n, n, 0)
    return mine + pair(other)


def both(x, axis):
    other = pair(x)
    first = lax.axis_index("c") == 0
    return jnp.where(
        first, jnp.concatenate([x, other], axis), jnp.concatenate([other, x], axis)
    )


def gram_of(zt):
    return jnp.dot(zt, zt.T, precision=HIGH)


def packed(g):
    n = g.shape[0] * g.shape[1] // 128
    return g.reshape(n, 128)


def finish(zt, gram):
    lower = jnp.linalg.cholesky(gram)
    return jax.scipy.linalg.solve_triangular(lower, zt, lower=True)


def on_device(field, init_y, init_t, sketch_x, sketch_y, sketch_t):
    rows_x, rows_y, rows_t = field.shape
    r3 = init_t.shape[1]
    r2 = init_y.shape[1]
    r1 = sketch_x.shape[1]
    w = jnp.einsum("xyt,tc->cxy", field, init_t, precision=MID)
    s_x = jnp.einsum("ya,ack->cyk", init_y, sketch_x.reshape(r2, r3, r1), precision=HIGH)
    zx = jnp.einsum("cxy,cyk->kx", w, s_x, precision=MID)
    zx = total(zx + pair(zx), ("z", "l"))
    gx = total(packed(gram_of(zx)), ("y", "h")).reshape(r1, r1)
    qx = finish(zx, gx)

    v = jnp.einsum("bck,bx->ckx", sketch_y.reshape(r1, r3, r2), qx, precision=HIGH)
    zy = jnp.einsum("ckx,cxy->ky", v, w, precision=MID)
    zy = both(total(half_sum(zy), ("y", "h", "l")), 0)
    gy = total(packed(gram_of(zy)), ("z",)).reshape(r2, r2)
    qy = finish(zy, gy)

    w_x = jnp.einsum("xyt,bx->byt", field, qx, precision=MID)
    part = jnp.einsum("byt,ay->bat", w_x, qy, precision=MID)
    zt = jnp.einsum("bat,bak->kt", part, sketch_t.reshape(r1, r2, r3), precision=MID)
    zt = total(zt, ("y", "h", "z"))
    gt = packed(gram_of(zt))
    gt = gt + pair(gt)
    gt = (gt + lax.ppermute(gt, "l", [(0, 1), (1, 0)])).reshape(r3, r3)
    lower = jnp.linalg.cholesky(gt)
    qt = jax.scipy.linalg.solve_triangular(lower, zt, lower=True)
    core = jnp.einsum("bat,kt->abk", part, zt, precision=MID)
    core = half_sum(core)
    core = core.transpose(1, 0, 2).reshape(r1, -1, 128)
    piece = lax.all_to_all(core, ("y", "h", "z", "l"), 0, 0).sum(0).reshape(-1, r3)
    piece = jax.scipy.linalg.solve_triangular(lower, piece.T, lower=True).T
    piece = spread(piece.reshape(-1, 128), ("y", "h", "z", "l"))
    core = both(piece.reshape(r1, -1), 1)
    total_x = rows_x * lax.axis_size(("y", "h"))
    total_y = rows_y * lax.axis_size("z")
    total_t = rows_t * lax.axis_size(("l", "c"))
    return (
        qx.T * math.sqrt(total_x),
        qy.T * math.sqrt(total_y),
        qt.T * math.sqrt(total_t),
        core,
    )


def solution(mesh):
    fine = Mesh(mesh.devices.reshape(4, 2, 4, 2, 2), ("y", "h", "z", "l", "c"))
    gx, gy, ta = ("y", "h"), "z", ("l", "c")
    in_specs = (P(gx, gy, ta), P(gy, None), P(ta, None), P(), P(), P())
    out_specs = (P(gx, None), P(gy, None), P(ta, None), P())
    return jax.shard_map(
        on_device, mesh=fine, in_specs=in_specs, out_specs=out_specs, check_vma=False
    )
```

```python
import math

import jax
import jax.numpy as jnp
from jax import lax
from jax.experimental import pallas as pl
from jax.experimental.pallas import tpu as pltpu
from jax.sharding import Mesh, PartitionSpec as P

HIGH = lax.Precision.HIGHEST
F32 = jnp.float32
BF16 = jnp.bfloat16
VMEM = pl.BlockSpec(memory_space=pltpu.VMEM)
HBM = pl.BlockSpec(memory_space=pltpu.HBM)
SMEM = pl.BlockSpec(memory_space=pltpu.SMEM)
MOST = 61 * 1024 * 1024
BIG = 58 * 1024 * 1024
MIDDLE = 4 * 1024 * 1024


def room(size):
    return pltpu.CompilerParams(vmem_limit_bytes=size)


def split(x):
    hi = x.astype(BF16)
    return hi, (x - hi.astype(F32)).astype(BF16)


def twice(x):
    hi, lo = split(x)
    return jnp.concatenate([jnp.concatenate([hi, hi], 1), jnp.concatenate([lo, lo], 1)], 0)


def dot(a, b, da=1, db=0, precision=None):
    return lax.dot_general(
        a, b, (((da,), (db,)), ((), ())), precision=precision, preferred_element_type=F32
    )


def tree_sum(parts):
    parts = list(parts)
    while len(parts) > 1:
        even = [parts[i] + parts[i + 1] for i in range(0, len(parts) - 1, 2)]
        parts = even + parts[len(even) * 2 :]
    return parts[0]


def cholesky_inverse(g):
    n = g.shape[0]
    nb = n // 8
    lane = lax.broadcasted_iota(jnp.int32, (8, 128), 1)
    sub = lax.broadcasted_iota(jnp.int32, (8, 128), 0)
    blocks = []
    for k in range(nb):
        eye = (lane - n == sub + 8 * k).astype(F32)
        wide = jnp.concatenate([g[8 * k : 8 * k + 8, :], jnp.zeros((8, 128 - n), F32)], 1)
        blocks.append(jnp.where(lane < n, wide, eye))
    out = []
    for kb in range(nb):
        rows = blocks[kb]
        cols = [
            jnp.broadcast_to(rows[:, 8 * kb + j : 8 * kb + j + 1], (8, 128)) for j in range(8)
        ]
        done = rows
        for p in range(8):
            inv = 1.0 / cols[p][p : p + 1, :]
            at = sub == p
            done = jnp.where(at, rows * lax.rsqrt(cols[p]), done)
            pivot = rows[p : p + 1, :] * inv
            rows = jnp.where(at, pivot, rows - cols[p] * pivot)
            for j in range(p + 1, 8):
                c = cols[j][p : p + 1, :] * inv
                cols[j] = jnp.where(at, c, cols[j] - cols[p] * c)
        out.append(done)
        for m in range(kb + 1, nb):
            b = blocks[m]
            blocks[m] = b - tree_sum(
                [b[:, 8 * kb + j : 8 * kb + j + 1] * rows[j : j + 1, :] for j in range(8)]
            )
    return jnp.concatenate(out, 0)[:, n : 2 * n]


def fold(g):
    return jnp.concatenate([g[:32], g[32:]], 1)


def unfold(g):
    return jnp.concatenate([g[:, :64], g[:, 64:]], 0)


def first_kernel(field, init_t, init_y, sketch, w, z, held, pair_w, lhs, turned, proj, sems, out_sems):
    nx, ny, nt = held.shape
    r3, r2, k = init_t.shape[0], init_y.shape[0], sketch.shape[0]
    chunks = sems.shape[0]
    rows = nx // chunks

    def copy(i):
        s = pl.ds(i * rows, rows)
        return pltpu.make_async_copy(field.at[s], held.at[s], sems.at[i])

    def copy_out(i, part):
        s = pl.ds(pl.multiple_of(i * rows + part * nx, 16), rows)
        return pltpu.make_async_copy(pair_w.at[:, s, :], w.at[:, s, :], out_sems.at[i, part])

    for i in range(chunks):
        copy(i).start()
    lhs[...] = twice(init_t[...])
    for i in range(0, r2 * r3, 128):
        turned[i : i + 128, :] = sketch[:, i : i + 128].T
    hi, lo = split(init_y[...])
    rhs = jnp.concatenate([hi, hi, lo, lo], 0)
    for c in range(r3):
        hi, lo = split(turned[pl.ds(c, r2, stride=r3), :].T)
        hi, lo = split(dot(jnp.concatenate([hi, lo, hi, lo], 1), rhs))
        proj[c, :k, :] = hi
        proj[c, k:, :] = lo

    def chunk(i, _):
        copy(i).wait()
        groups = []
        for x8 in range(0, rows, 8):
            outs = []
            for x in range(8):
                hi, lo = split(held[i * rows + x8 + x])
                o = dot(lhs[...], jnp.concatenate([hi, lo], 1), 1, 1)
                outs.append(o[:r3] + o[r3:])
            groups.append(jnp.swapaxes(jnp.stack(outs, 0), 0, 1))
        hi, lo = split(jnp.concatenate(groups, 1))
        at = pl.multiple_of(i * rows, 16)
        pair_w[:, pl.ds(at, rows), :] = hi
        pair_w[:, pl.ds(pl.multiple_of(at + nx, 16), rows), :] = lo
        copy_out(i, 0).start()
        copy_out(i, 1).start()
        return 0

    lax.fori_loop(0, chunks, chunk, 0)
    acc = dot(proj[0], pair_w[0], 1, 1)
    for c in range(1, r3):
        acc += dot(proj[c], pair_w[c], 1, 1)
    z[...] = (acc[k:, :nx] + acc[:k, nx:] + acc[k:, nx:]) + acc[:k, :nx]
    for i in range(chunks):
        copy_out(i, 0).wait()
        copy_out(i, 1).wait()


def first(field, init_t, init_y, sketch):
    nx, ny, nt = field.shape
    r3, r2, k = init_t.shape[0], init_y.shape[0], sketch.shape[0]
    return pl.pallas_call(
        first_kernel,
        in_specs=[HBM, VMEM, VMEM, VMEM],
        out_specs=[HBM, VMEM],
        out_shape=[
            jax.ShapeDtypeStruct((r3, 2 * nx, ny), BF16),
            jax.ShapeDtypeStruct((k, nx), F32),
        ],
        scratch_shapes=[
            pltpu.VMEM((nx, ny, nt), F32),
            pltpu.VMEM((r3, 2 * nx, ny), BF16),
            pltpu.VMEM((2 * r3, 2 * nt), BF16),
            pltpu.VMEM((r2 * r3, k), F32),
            pltpu.VMEM((r3, 2 * k, ny), BF16),
            pltpu.SemaphoreType.DMA((8,)),
            pltpu.SemaphoreType.DMA((8, 2)),
        ],
        compiler_params=room(BIG),
        cost_estimate=pl.CostEstimate(
            flops=8 * nx * ny * nt * r3, bytes_accessed=nx * ny * nt * 4, transcendentals=0
        ),
    )(field, init_t, init_y, sketch)


def gram_kernel(parts, z, gram):
    total = tree_sum([parts[i] for i in range(parts.shape[0])])
    z[...] = total
    g = fold(dot(total, total, 1, 1, HIGH))
    for i in range(gram.shape[0]):
        gram[i] = g


def gram_of(parts, copies):
    k, n = parts.shape[1:]
    return pl.pallas_call(
        gram_kernel,
        in_specs=[VMEM],
        out_specs=[VMEM, VMEM],
        out_shape=[
            jax.ShapeDtypeStruct((k, n), F32),
            jax.ShapeDtypeStruct((copies, k * k // 128, 128), F32),
        ],
        compiler_params=room(MIDDLE),
    )(parts)


def sketch_y_kernel(sketch, out, turned):
    k = sketch.shape[0]
    r3 = out.shape[0] // k
    r1 = sketch.shape[1] // r3
    for i in range(0, r1 * r3, 128):
        turned[i : i + 128, :] = sketch[:, i : i + 128].T
    for c in range(r3):
        hi, lo = split(turned[pl.ds(c, r1, stride=r3), :].T)
        out[c * k : (c + 1) * k, :] = jnp.concatenate([hi, lo, hi, lo], 1)


def prepared_y(sketch, r3):
    k, n = sketch.shape
    return pl.pallas_call(
        sketch_y_kernel,
        in_specs=[VMEM],
        out_specs=VMEM,
        out_shape=jax.ShapeDtypeStruct((r3 * k, 4 * n // r3), BF16),
        scratch_shapes=[pltpu.VMEM((n, k), F32)],
        compiler_params=room(MIDDLE),
        cost_estimate=pl.CostEstimate(flops=10**7, bytes_accessed=2 * 10**6, transcendentals=0),
    )(sketch)


def second_kernel(scale, core_id, grams, z, sk, w, q, factor, mine, other, pair_w, sems):
    r3 = pair_w.shape[0]
    each = r3 // sems.shape[0]

    def copy(i):
        s = pl.ds(i * each, each)
        return pltpu.make_async_copy(w.at[s], pair_w.at[s], sems.at[i])

    for i in range(r3 // each):
        copy(i).start()
    g = unfold(tree_sum([grams[i] for i in range(grams.shape[0])]))
    qv = dot(cholesky_inverse(g), z[...], 1, 0, HIGH)
    q[...] = qv
    factor[...] = qv * scale
    hi, lo = split(qv)
    v = dot(sk[...], jnp.concatenate([hi, hi, lo, lo], 0))
    half = mine.shape[0]
    k = 2 * half
    acc = None
    for c in range(r3):
        if c % each == 0:
            copy(c // each).wait()
        o = dot(twice(v[c * k : (c + 1) * k]), pair_w[c])
        acc = o if acc is None else acc + o
    zy = acc[k:] + acc[:k]
    first = core_id[0] == 0
    mine[...] = jnp.where(first, zy[:half], zy[half:])
    other[...] = jnp.where(first, zy[half:], zy[:half])


def second(core_id, grams, z, sk, pair_w, scale):
    r1, nx = z.shape
    r3, _, ny = pair_w.shape
    half = jax.ShapeDtypeStruct((sk.shape[0] // r3 // 2, ny), F32)
    return pl.pallas_call(
        lambda *a: second_kernel(scale, *a),
        in_specs=[SMEM, VMEM, VMEM, VMEM, HBM],
        out_specs=[VMEM] * 4,
        out_shape=[
            jax.ShapeDtypeStruct((r1, nx), F32),
            jax.ShapeDtypeStruct((r1, nx), F32),
            half,
            half,
        ],
        scratch_shapes=[pltpu.VMEM(pair_w.shape, BF16), pltpu.SemaphoreType.DMA((4,))],
        compiler_params=room(MOST),
    )(core_id, grams, z, sk, pair_w)


def contract_x_kernel(q, field, wx, held, out, lhs, sems, out_sems):
    nx, ny, nt = held.shape
    r1 = q.shape[0]
    chunks = sems.shape[0]
    rows = ny // chunks

    def copy(i):
        s = pl.ds(pl.multiple_of(i * rows, 8), rows)
        return pltpu.make_async_copy(field.at[:, s, :], held.at[:, s, :], sems.at[i])

    def copy_out(i):
        s = pl.ds(pl.multiple_of(i * rows, 8), rows)
        return pltpu.make_async_copy(out.at[:, s, :], wx.at[:, s, :], out_sems.at[i])

    for i in range(chunks):
        copy(i).start()
    lhs[...] = twice(q[...])

    def chunk(i, _):
        copy(i).wait()
        for y8 in range(0, rows, 8):
            at = pl.multiple_of(i * rows + y8, 8)
            f = jnp.swapaxes(held[:, pl.ds(at, 8), :], 0, 1)
            outs = []
            for y in range(0, 8, 2):
                h0, l0 = split(f[y])
                h1, l1 = split(f[y + 1])
                rhs = jnp.concatenate(
                    [jnp.concatenate([h0, h1], 1), jnp.concatenate([l0, l1], 1)], 0
                )
                o = dot(lhs[...], rhs)
                o = o[r1:] + o[:r1]
                outs += [o[:, :nt], o[:, nt:]]
            out[:, pl.ds(at, 8), :] = jnp.swapaxes(jnp.stack(outs, 0), 0, 1)
        copy_out(i).start()
        return 0

    lax.fori_loop(0, chunks, chunk, 0)
    for i in range(chunks):
        copy_out(i).wait()


def contract_x(q, field):
    nx, ny, nt = field.shape
    r1 = q.shape[0]
    return pl.pallas_call(
        contract_x_kernel,
        in_specs=[VMEM, HBM],
        out_specs=HBM,
        out_shape=jax.ShapeDtypeStruct((r1, ny, nt), F32),
        scratch_shapes=[
            pltpu.VMEM((nx, ny, nt), F32),
            pltpu.VMEM((r1, ny, nt), F32),
            pltpu.VMEM((2 * r1, 2 * nx), BF16),
            pltpu.SemaphoreType.DMA((8,)),
            pltpu.SemaphoreType.DMA((8,)),
        ],
        compiler_params=room(BIG),
        cost_estimate=pl.CostEstimate(
            flops=8 * nx * ny * nt * r1, bytes_accessed=nx * ny * nt * 6, transcendentals=0
        ),
    )(q, field)


def third_kernel(scale, grams, z, sketch, w_hbm, factor, part, zt, wx, sems):
    r1, ny, nt = wx.shape
    r2 = z.shape[0]
    chunks = sems.shape[0]
    rows = r1 // chunks

    def copy(i):
        s = pl.ds(i * rows, rows)
        return pltpu.make_async_copy(w_hbm.at[s], wx.at[s], sems.at[i])

    for i in range(chunks):
        copy(i).start()
    g = unfold(tree_sum([grams[i] for i in range(grams.shape[0])]))
    qv = dot(cholesky_inverse(g), z[...], 1, 0, HIGH)
    factor[...] = qv * scale
    hi, lo = split(qv)
    lhs = jnp.concatenate([hi, lo], 0)
    k = sketch.shape[0]
    group = rows

    def step(i, acc):
        copy(i).wait()
        for b in range(group):
            hi, lo = split(wx[i * group + b])
            o = dot(lhs, jnp.concatenate([hi, lo], 1))
            o = (o[r2:, :nt] + o[:r2, nt:] + o[r2:, nt:]) + o[:r2, :nt]
            hi, lo = split(o)
            at = pl.multiple_of(i * group * r2 + b * r2, r2)
            part[pl.ds(at, r2), :] = jnp.concatenate([hi, lo], 1)
        s = pl.ds(pl.multiple_of(i * group * r2, group * r2), group * r2)
        hi, lo = split(sketch[:, s])
        return acc + dot(jnp.concatenate([hi, lo], 0), part[s, :])

    acc = lax.fori_loop(0, r1 // group, step, jnp.zeros((2 * k, 2 * nt), F32))
    total = (acc[k:, :nt] + acc[:k, nt:] + acc[k:, nt:]) + acc[:k, :nt]
    for i in range(zt.shape[0]):
        zt[i] = total


def third(grams, z, sketch, wx, scale, copies):
    r2, ny = z.shape
    r1, _, nt = wx.shape
    k = sketch.shape[0]
    return pl.pallas_call(
        lambda *a: third_kernel(scale, *a),
        in_specs=[VMEM, VMEM, VMEM, HBM],
        out_specs=[VMEM] * 3,
        out_shape=[
            jax.ShapeDtypeStruct((r2, ny), F32),
            jax.ShapeDtypeStruct((r1 * r2, 2 * nt), BF16),
            jax.ShapeDtypeStruct((copies, k, nt), F32),
        ],
        scratch_shapes=[pltpu.VMEM(wx.shape, F32), pltpu.SemaphoreType.DMA((16,))],
        compiler_params=room(BIG),
    )(grams, z, sketch, wx)


def core_kernel(core_id, parts, part, z, gram, mine, other):
    total = tree_sum([parts[i] for i in range(parts.shape[0])])
    z[...] = total
    gram[...] = dot(total, total, 1, 1, HIGH)
    k = total.shape[0]
    lhs = twice(total)
    group = lax.broadcasted_iota(jnp.int32, (8, 128), 1) // 32
    first = core_id[0] == 0
    for i in range(part.shape[0] // 256):
        o = dot(lhs, part[i * 256 : (i + 1) * 256, :], 1, 1)
        o = o[k:] + o[:k]
        for j in range(2):
            v = [o[8 * g : 8 * g + 8, 128 * j : 128 * j + 128] for g in range(4)]
            slots = []
            for s in range(4):
                t = None
                for g in range(4):
                    shift = (g - s) * 32 % 128
                    u = pltpu.roll(v[g], shift, 1) if shift else v[g]
                    t = u if t is None else jnp.where(group == g, u, t)
                slots.append(t)
            for b in range(2):
                at = i * 4 + j * 2 + b
                mine[at] = jnp.where(first, slots[2 * b], slots[2 * b + 1])
                other[at] = jnp.where(first, slots[2 * b + 1], slots[2 * b])


def core_terms(core_id, parts, part, r1):
    k, nt = parts.shape[1:]
    slots = jax.ShapeDtypeStruct((r1, 8, 128), F32)
    return pl.pallas_call(
        core_kernel,
        in_specs=[SMEM, VMEM, VMEM],
        out_specs=[VMEM] * 4,
        out_shape=[
            jax.ShapeDtypeStruct((k, nt), F32),
            jax.ShapeDtypeStruct((k, k), F32),
            slots,
            slots,
        ],
        compiler_params=room(MIDDLE),
    )(core_id, parts, part)


def scale_kernel(scale, gram0, gram1, z, pieces, factor, out, held):
    inv = cholesky_inverse(gram0[...] + gram1[...])
    factor[...] = dot(inv, z[...], 1, 0, HIGH) * scale
    piece = tree_sum([pieces[i] for i in range(pieces.shape[0])])
    x = jnp.concatenate([piece[:, 32 * g : 32 * g + 32] for g in range(4)], 0)
    held[...] = dot(x, inv, 0, 1, HIGH)
    row = jnp.concatenate([held[pl.ds(s, 8, stride=4), :] for s in range(4)], 1)
    for i in range(out.shape[0]):
        out[i] = row


def scaled(gram0, gram1, z, pieces, scale):
    k, nt = z.shape
    return pl.pallas_call(
        lambda *a: scale_kernel(scale, *a),
        in_specs=[VMEM] * 4,
        out_specs=[VMEM] * 2,
        out_shape=[
            jax.ShapeDtypeStruct((k, nt), F32),
            jax.ShapeDtypeStruct(pieces.shape, F32),
        ],
        scratch_shapes=[pltpu.VMEM((k, k), F32)],
        compiler_params=room(MIDDLE),
    )(gram0, gram1, z, pieces)


def join_kernel(core_id, own, other, out):
    first = core_id[0] == 0
    half = out.shape[1] // 2
    for r in range(own.shape[1]):
        a = own[:, r, :]
        b = other[:, r, :]
        out[:, r * 128 : (r + 1) * 128] = jnp.where(first, a, b)
        out[:, half + r * 128 : half + (r + 1) * 128] = jnp.where(first, b, a)


def joined(core_id, own, other):
    n = own.shape[0]
    return pl.pallas_call(
        join_kernel,
        in_specs=[SMEM, VMEM, VMEM],
        out_specs=VMEM,
        out_shape=jax.ShapeDtypeStruct((n, 2 * 8 * 128), F32),
        compiler_params=room(MIDDLE),
    )(core_id, own, other)


def pair(x):
    return lax.ppermute(x, "c", [(0, 1), (1, 0)])


def exchange(x, axes):
    return lax.all_to_all(x, axes, 0, 0)


def spread(x, axes):
    n = math.prod(lax.axis_size(a) for a in axes)
    return exchange(jnp.broadcast_to(x, (n,) + x.shape), axes)


def both(x, axis):
    other = pair(x)
    first = lax.axis_index("c") == 0
    return jnp.where(
        first, jnp.concatenate([x, other], axis), jnp.concatenate([other, x], axis)
    )


def on_device(field, init_y, init_t, sketch_x, sketch_y, sketch_t):
    rows_x, rows_y, rows_t = field.shape
    r3 = init_t.shape[1]
    r1 = sketch_x.shape[1]
    scale_x = math.sqrt(rows_x * lax.axis_size(("y", "h")))
    scale_y = math.sqrt(rows_y * lax.axis_size("z"))
    scale_t = math.sqrt(rows_t * lax.axis_size(("l", "c")))
    core_id = lax.axis_index("c").astype(jnp.int32).reshape(1)

    pair_w, zx = first(field, init_t.T, init_y.T, sketch_x.T)
    zx, gx = gram_of(spread(zx + pair(zx), ("z", "l")), 8)
    sk_y = prepared_y(sketch_y.T, r3)
    qx, factor_x, mine, other = second(
        core_id, exchange(gx, ("y", "h")), zx, sk_y, pair_w, scale_x
    )
    wx = contract_x(qx, field)
    zy = spread(mine + pair(other), ("y", "h", "l")).sum(0)
    zy, wx = lax.optimization_barrier((zy, wx))
    zy = both(zy, 0)
    zy, gy = gram_of(zy[None], 4)
    factor_y, part, zt = third(exchange(gy, ("z",)), zy, sketch_t.T, wx, scale_y, 32)
    zt, gt, mine, other = core_terms(core_id, exchange(zt, ("y", "h", "z")), part, r1)
    gt = gt + pair(gt)
    gt_other = lax.ppermute(gt, "l", [(0, 1), (1, 0)])
    pieces = exchange(mine + pair(other), ("y", "h", "z", "l"))
    factor_t, piece = scaled(gt, gt_other, zt, pieces, scale_t)
    piece = exchange(piece, ("y", "h", "z", "l"))
    core = joined(core_id, piece, pair(piece))
    return factor_x.T, factor_y.T, factor_t.T, core


def solution(mesh):
    fine = Mesh(mesh.devices.reshape(4, 2, 4, 2, 2), ("y", "h", "z", "l", "c"))
    gx, gy, ta = ("y", "h"), "z", ("l", "c")
    in_specs = (P(gx, gy, ta), P(gy, None), P(ta, None), P(), P(), P())
    out_specs = (P(gx, None), P(gy, None), P(ta, None), P())
    return jax.shard_map(
        on_device, mesh=fine, in_specs=in_specs, out_specs=out_specs, check_vma=False
    )
```

```python
import math

import jax
import jax.numpy as jnp
from jax import lax
from jax.experimental import pallas as pl
from jax.experimental.pallas import tpu as pltpu
from jax.sharding import Mesh, PartitionSpec as P

HIGH = lax.Precision.HIGHEST
F32 = jnp.float32
BF16 = jnp.bfloat16
VMEM = pl.BlockSpec(memory_space=pltpu.VMEM)
HBM = pl.BlockSpec(memory_space=pltpu.HBM)
SMEM = pl.BlockSpec(memory_space=pltpu.SMEM)
MOST = 58 * 1024 * 1024
BIG = 49 * 1024 * 1024
AHEAD = 4
MIDDLE = 4 * 1024 * 1024


def room(size):
    return pltpu.CompilerParams(vmem_limit_bytes=size)


def split(x):
    hi = x.astype(BF16)
    return hi, (x - hi.astype(F32)).astype(BF16)


def twice(x):
    hi, lo = split(x)
    return jnp.concatenate([jnp.concatenate([hi, hi], 1), jnp.concatenate([lo, lo], 1)], 0)


def dot(a, b, da=1, db=0, precision=None):
    return lax.dot_general(
        a, b, (((da,), (db,)), ((), ())), precision=precision, preferred_element_type=F32
    )


def tree_sum(parts):
    parts = list(parts)
    while len(parts) > 1:
        even = [parts[i] + parts[i + 1] for i in range(0, len(parts) - 1, 2)]
        parts = even + parts[len(even) * 2 :]
    return parts[0]


def cholesky_inverse(g):
    n = g.shape[0]
    nb = n // 8
    lane = lax.broadcasted_iota(jnp.int32, (8, 128), 1)
    sub = lax.broadcasted_iota(jnp.int32, (8, 128), 0)
    blocks = []
    for k in range(nb):
        eye = (lane - n == sub + 8 * k).astype(F32)
        wide = jnp.concatenate([g[8 * k : 8 * k + 8, :], jnp.zeros((8, 128 - n), F32)], 1)
        blocks.append(jnp.where(lane < n, wide, eye))
    out = []
    for kb in range(nb):
        rows = blocks[kb]
        cols = [
            jnp.broadcast_to(rows[:, 8 * kb + j : 8 * kb + j + 1], (8, 128)) for j in range(8)
        ]
        done = rows
        for p in range(8):
            inv = 1.0 / cols[p][p : p + 1, :]
            at = sub == p
            done = jnp.where(at, rows * lax.rsqrt(cols[p]), done)
            pivot = rows[p : p + 1, :] * inv
            rows = jnp.where(at, pivot, rows - cols[p] * pivot)
            for j in range(p + 1, 8):
                c = cols[j][p : p + 1, :] * inv
                cols[j] = jnp.where(at, c, cols[j] - cols[p] * c)
        out.append(done)
        for m in range(kb + 1, nb):
            b = blocks[m]
            blocks[m] = b - tree_sum(
                [b[:, 8 * kb + j : 8 * kb + j + 1] * rows[j : j + 1, :] for j in range(8)]
            )
    return jnp.concatenate(out, 0)[:, n : 2 * n]


def fold(g):
    return jnp.concatenate([g[:32], g[32:]], 1)


def unfold(g):
    return jnp.concatenate([g[:, :64], g[:, 64:]], 0)


def first_kernel(
    field, init_t, init_y, sketch, w, z, held, pair_w, in_t, in_y, in_s, lhs, unfolded, sems, out_sems
):
    nx, ny, nt = held.shape
    r3, r2, k = init_t.shape[0], init_y.shape[0], sketch.shape[0]
    chunks = out_sems.shape[0]
    rows = nx // chunks

    def copy(i):
        s = pl.ds(i * rows, rows)
        return pltpu.make_async_copy(field.at[s], held.at[s], sems.at[i])

    def copy_out(i, part):
        s = pl.ds(pl.multiple_of(i * rows + part * nx, 16), rows)
        return pltpu.make_async_copy(
            pair_w.at[:, s, :], w.at[pl.ds(0, r3), s, :], out_sems.at[i, part]
        )

    small = [
        pltpu.make_async_copy(init_t, in_t, sems.at[chunks]),
        pltpu.make_async_copy(init_y, in_y, sems.at[chunks + 1]),
        pltpu.make_async_copy(sketch, in_s, sems.at[chunks + 2]),
    ]
    for c in small:
        c.start()
    for i in range(AHEAD):
        copy(i).start()
    small[0].wait()
    lhs[...] = twice(in_t[...])

    def chunk(i, _):
        copy(i).wait()

        @pl.when(i + AHEAD < chunks)
        def _():
            copy(i + AHEAD).start()

        groups = []
        for x8 in range(0, rows, 8):
            outs = []
            for x in range(8):
                hi, lo = split(held[i * rows + x8 + x])
                o = dot(lhs[...], jnp.concatenate([hi, lo], 1), 1, 1)
                outs.append(o[:r3] + o[r3:])
            groups.append(jnp.swapaxes(jnp.stack(outs, 0), 0, 1))
        hi, lo = split(jnp.concatenate(groups, 1))
        at = pl.multiple_of(i * rows, 16)
        pair_w[:, pl.ds(at, rows), :] = hi
        pair_w[:, pl.ds(pl.multiple_of(at + nx, 16), rows), :] = lo
        copy_out(i, 0).start()
        copy_out(i, 1).start()
        return 0

    lax.fori_loop(0, chunks, chunk, 0)
    small[1].wait()
    small[2].wait()
    hi, lo = split(in_y[...])
    left = jnp.concatenate([hi, lo], 0)
    for c8 in range(0, r3, 8):
        outs = []
        for c in range(c8, c8 + 8):
            o = dot(left, pair_w[c], 1, 1)
            outs.append((o[r2:, :nx] + o[:r2, nx:] + o[r2:, nx:]) + o[:r2, :nx])
        unfolded[:, c8 : c8 + 8, :] = jnp.swapaxes(jnp.stack(outs, 0), 0, 1)
    acc = None
    for a in range(0, r2, 8):
        hi, lo = split(unfolded[a : a + 8].reshape(8 * r3, nx))
        sh, sl = split(in_s[:, a * r3 : (a + 8) * r3])
        o = dot(jnp.concatenate([sh, sl], 0), jnp.concatenate([hi, lo], 1))
        acc = o if acc is None else acc + o
    total = (acc[k:, :nx] + acc[:k, nx:] + acc[k:, nx:]) + acc[:k, :nx]
    for i in range(z.shape[0]):
        z[i] = total
    for i in range(chunks):
        copy_out(i, 0).wait()
        copy_out(i, 1).wait()


def first(field, init_t, init_y, sketch, copies):
    nx, ny, nt = field.shape
    r3, r2, k = init_t.shape[0], init_y.shape[0], sketch.shape[0]
    return pl.pallas_call(
        first_kernel,
        in_specs=[HBM, HBM, HBM, HBM],
        out_specs=[HBM, VMEM],
        out_shape=[
            jax.ShapeDtypeStruct((4 * r3, 2 * nx, ny), BF16),
            jax.ShapeDtypeStruct((copies, k, nx), F32),
        ],
        scratch_shapes=[
            pltpu.VMEM((nx, ny, nt), F32),
            pltpu.VMEM((r3, 2 * nx, ny), BF16),
            pltpu.VMEM(init_t.shape, F32),
            pltpu.VMEM(init_y.shape, F32),
            pltpu.VMEM(sketch.shape, F32),
            pltpu.VMEM((2 * r3, 2 * nt), BF16),
            pltpu.VMEM((r2, r3, nx), F32),
            pltpu.SemaphoreType.DMA((11,)),
            pltpu.SemaphoreType.DMA((8, 2)),
        ],
        compiler_params=room(MOST),
        cost_estimate=pl.CostEstimate(
            flops=8 * nx * ny * nt * r3, bytes_accessed=nx * ny * nt * 4, transcendentals=0
        ),
    )(field, init_t, init_y, sketch)


def gram_kernel(*refs):
    *parts, z, gram = refs
    total = sum(tree_sum([p[i] for i in range(p.shape[0])]) for p in parts)
    z[...] = total
    g = fold(dot(total, total, 1, 1, HIGH))
    for i in range(gram.shape[0]):
        gram[i] = g


def gram_of(copies, *parts):
    k, n = parts[0].shape[1:]
    return pl.pallas_call(
        gram_kernel,
        in_specs=[VMEM] * len(parts),
        out_specs=[VMEM, VMEM],
        out_shape=[
            jax.ShapeDtypeStruct((k, n), F32),
            jax.ShapeDtypeStruct((copies, k * k // 128, 128), F32),
        ],
        compiler_params=room(MIDDLE),
    )(*parts)


def sketch_y_kernel(sketch, out, turned):
    k = sketch.shape[0]
    r3 = out.shape[0] // k
    r1 = sketch.shape[1] // r3
    for i in range(0, r1 * r3, 128):
        turned[i : i + 128, :] = sketch[:, i : i + 128].T
    for c in range(r3):
        hi, lo = split(turned[pl.ds(c, r1, stride=r3), :].T)
        out[c * k : (c + 1) * k, :] = jnp.concatenate([hi, lo, hi, lo], 1)


def prepared_y(sketch, r3):
    k, n = sketch.shape
    return pl.pallas_call(
        sketch_y_kernel,
        in_specs=[VMEM],
        out_specs=VMEM,
        out_shape=jax.ShapeDtypeStruct((r3 * k, 4 * n // r3), BF16),
        scratch_shapes=[pltpu.VMEM((n, k), F32)],
        compiler_params=room(MIDDLE),
        cost_estimate=pl.CostEstimate(flops=10**7, bytes_accessed=2 * 10**6, transcendentals=0),
    )(sketch)


def second_kernel(scale, core_id, grams, z, sk, w, q, factor, mine, other, pair_w, sems):
    r3 = pair_w.shape[0]
    each = r3 // sems.shape[0]

    def copy(i):
        s = pl.ds(i * each, each)
        return pltpu.make_async_copy(w.at[s], pair_w.at[s], sems.at[i])

    def start(i, _):
        copy(i).start()
        return 0

    lax.fori_loop(0, r3 // each, start, 0)
    g = unfold(tree_sum([grams[i] for i in range(grams.shape[0])]))
    qv = dot(cholesky_inverse(g), z[...], 1, 0, HIGH)
    q[...] = qv
    factor[...] = qv * scale
    hi, lo = split(qv)
    v = dot(sk[...], jnp.concatenate([hi, hi, lo, lo], 0))
    half = mine.shape[0]
    k = 2 * half
    acc = None
    for c in range(r3):
        if c % each == 0:
            copy(c // each).wait()
        o = dot(twice(v[c * k : (c + 1) * k]), pair_w[c])
        acc = o if acc is None else acc + o
    zy = acc[k:] + acc[:k]
    first = core_id[0] == 0
    mine[...] = jnp.where(first, zy[:half], zy[half:])
    other[...] = jnp.where(first, zy[half:], zy[:half])


def second(core_id, grams, z, sk, w, scale, r3):
    r1, nx = z.shape
    ny = w.shape[2]
    half = jax.ShapeDtypeStruct((sk.shape[0] // r3 // 2, ny), F32)
    return pl.pallas_call(
        lambda *a: second_kernel(scale, *a),
        in_specs=[SMEM, VMEM, VMEM, VMEM, HBM],
        out_specs=[VMEM] * 4,
        out_shape=[
            jax.ShapeDtypeStruct((r1, nx), F32),
            jax.ShapeDtypeStruct((r1, nx), F32),
            half,
            half,
        ],
        scratch_shapes=[
            pltpu.VMEM((r3, 2 * nx, ny), BF16),
            pltpu.SemaphoreType.DMA((4,)),
        ],
        compiler_params=room(BIG),
    )(core_id, grams, z, sk, w)


def contract_x_kernel(q, field, wx, held, out, lhs, sems, out_sems):
    nx, ny, nt = held.shape
    r1 = q.shape[0]
    chunks = sems.shape[0]
    rows = ny // chunks

    def copy(i):
        s = pl.ds(pl.multiple_of(i * rows, 8), rows)
        return pltpu.make_async_copy(field.at[:, s, :], held.at[:, s, :], sems.at[i])

    def copy_out(i):
        s = pl.ds(pl.multiple_of(i * rows, 8), rows)
        return pltpu.make_async_copy(
            out.at[:, s, :], wx.at[pl.ds(0, r1), s, :], out_sems.at[i]
        )

    for i in range(AHEAD):
        copy(i).start()
    lhs[...] = twice(q[...])

    def chunk(i, _):
        copy(i).wait()

        @pl.when(i + AHEAD < chunks)
        def _():
            copy(i + AHEAD).start()

        for y8 in range(0, rows, 8):
            at = pl.multiple_of(i * rows + y8, 8)
            f = jnp.swapaxes(held[:, pl.ds(at, 8), :], 0, 1)
            outs = []
            for y in range(0, 8, 2):
                h0, l0 = split(f[y])
                h1, l1 = split(f[y + 1])
                rhs = jnp.concatenate(
                    [jnp.concatenate([h0, h1], 1), jnp.concatenate([l0, l1], 1)], 0
                )
                o = dot(lhs[...], rhs)
                o = o[r1:] + o[:r1]
                outs += [o[:, :nt], o[:, nt:]]
            out[:, pl.ds(at, 8), :] = jnp.swapaxes(jnp.stack(outs, 0), 0, 1)
        copy_out(i).start()
        return 0

    lax.fori_loop(0, chunks, chunk, 0)
    for i in range(chunks):
        copy_out(i).wait()


def contract_x(q, field):
    nx, ny, nt = field.shape
    r1 = q.shape[0]
    chunks = ny // 32
    return pl.pallas_call(
        contract_x_kernel,
        in_specs=[VMEM, HBM],
        out_specs=HBM,
        out_shape=jax.ShapeDtypeStruct((2 * r1, ny, nt), F32),
        scratch_shapes=[
            pltpu.VMEM((nx, ny, nt), F32),
            pltpu.VMEM((r1, ny, nt), F32),
            pltpu.VMEM((2 * r1, 2 * nx), BF16),
            pltpu.SemaphoreType.DMA((chunks,)),
            pltpu.SemaphoreType.DMA((chunks,)),
        ],
        compiler_params=room(BIG),
        cost_estimate=pl.CostEstimate(
            flops=8 * nx * ny * nt * r1, bytes_accessed=nx * ny * nt * 6, transcendentals=0
        ),
    )(q, field)


def third_kernel(scale, g0, g1, g2, g3, z, sketch, wa, factor, part, zt, wx, sems):
    r1, ny, nt = wx.shape
    r2 = z.shape[0]
    chunks = sems.shape[0]
    rows = r1 // chunks

    def copy(i):
        s = pl.ds(i * rows, rows)
        return pltpu.make_async_copy(wa.at[s], wx.at[s], sems.at[i])

    def start(i, _):
        copy(i).start()
        return 0

    lax.fori_loop(0, chunks, start, 0)
    g = unfold((g0[...] + g1[...]) + (g2[...] + g3[...]))
    qv = dot(cholesky_inverse(g), z[...], 1, 0, HIGH)
    factor[...] = qv * scale
    hi, lo = split(qv)
    lhs = jnp.concatenate([hi, lo], 0)
    k = sketch.shape[0]
    group = 4

    def step(i, acc):
        copy(i).wait()
        for b in range(rows):
            hi, lo = split(wx[i * rows + b])
            o = dot(lhs, jnp.concatenate([hi, lo], 1))
            o = (o[r2:, :nt] + o[:r2, nt:] + o[r2:, nt:]) + o[:r2, :nt]
            hi, lo = split(o)
            at = pl.multiple_of((i * rows + b) * r2, r2)
            part[pl.ds(at, r2), :] = jnp.concatenate([hi, lo], 1)
        for b in range(0, rows, group):
            n = group * r2
            s = pl.ds(pl.multiple_of((i * rows + b) * r2, n), n)
            hi, lo = split(sketch[:, s])
            acc = acc + dot(jnp.concatenate([hi, lo], 0), part[s, :])
        return acc

    acc = jnp.zeros((2 * k, 2 * nt), F32)
    for i in range(chunks):
        acc = step(i, acc)
    total = (acc[k:, :nt] + acc[:k, nt:] + acc[k:, nt:]) + acc[:k, :nt]
    for i in range(zt.shape[0]):
        zt[i] = total


def third(grams, z, sketch, wa, scale, copies, r1):
    r2, ny = z.shape
    nt = wa.shape[2]
    k = sketch.shape[0]
    return pl.pallas_call(
        lambda *a: third_kernel(scale, *a),
        in_specs=[VMEM] * 6 + [HBM],
        out_specs=[VMEM] * 3,
        out_shape=[
            jax.ShapeDtypeStruct((r2, ny), F32),
            jax.ShapeDtypeStruct((r1 * r2, 2 * nt), BF16),
            jax.ShapeDtypeStruct((copies, k, nt), F32),
        ],
        scratch_shapes=[pltpu.VMEM((r1, ny, nt), F32), pltpu.SemaphoreType.DMA((2,))],
        compiler_params=room(BIG),
    )(*grams, z, sketch, wa)


def core_kernel(parts, part, z, gram, out):
    total = tree_sum([parts[i] for i in range(parts.shape[0])])
    z[...] = total
    gram[...] = dot(total, total, 1, 1, HIGH)
    k = total.shape[0]
    lhs = twice(total)
    group = lax.broadcasted_iota(jnp.int32, (8, 128), 1) // 32
    for i in range(part.shape[0] // 256):
        o = dot(lhs, part[i * 256 : (i + 1) * 256, :], 1, 1)
        o = o[k:] + o[:k]
        for j in range(2):
            v = [o[8 * g : 8 * g + 8, 128 * j : 128 * j + 128] for g in range(4)]
            for s in range(4):
                t = None
                for g in range(4):
                    shift = (g - s) * 32 % 128
                    u = pltpu.roll(v[g], shift, 1) if shift else v[g]
                    t = u if t is None else jnp.where(group == g, u, t)
                at = i * 4 + j * 2 + s // 2
                out[at, 8 * (s % 2) : 8 * (s % 2) + 8, :] = t


def core_terms(parts, part, r1):
    k, nt = parts.shape[1:]
    return pl.pallas_call(
        core_kernel,
        in_specs=[VMEM, VMEM],
        out_specs=[VMEM] * 3,
        out_shape=[
            jax.ShapeDtypeStruct((k, nt), F32),
            jax.ShapeDtypeStruct((k, k), F32),
            jax.ShapeDtypeStruct((r1, 16, 128), F32),
        ],
        compiler_params=room(MIDDLE),
    )(parts, part)


def inverse_kernel(scale, g0, g1, g2, g3, z, factor, inv):
    inv[...] = cholesky_inverse((g0[...] + g1[...]) + (g2[...] + g3[...]))
    factor[...] = dot(inv[...], z[...], 1, 0, HIGH) * scale


def last_factor(grams, z, scale):
    k, nt = z.shape
    return pl.pallas_call(
        lambda *a: inverse_kernel(scale, *a),
        in_specs=[VMEM] * 5,
        out_specs=[VMEM] * 2,
        out_shape=[jax.ShapeDtypeStruct((k, nt), F32), jax.ShapeDtypeStruct((k, k), F32)],
        compiler_params=room(MIDDLE),
        cost_estimate=pl.CostEstimate(flops=10**7, bytes_accessed=2 * 10**6, transcendentals=0),
    )(*grams, z)


def scale_kernel(core_id, inv, own, other, out, held):
    piece = own[...] + other[...]
    piece = jnp.where(core_id[0] == 0, piece[:8], piece[8:])
    x = jnp.concatenate([piece[:, 32 * g : 32 * g + 32] for g in range(4)], 0)
    held[...] = dot(x, inv[...], 0, 1, HIGH)
    row = jnp.concatenate([held[pl.ds(s, 8, stride=4), :] for s in range(4)], 1)
    for i in range(out.shape[0]):
        out[i] = row


def scaled(core_id, inv, own, other, copies):
    k = inv.shape[0]
    return pl.pallas_call(
        scale_kernel,
        in_specs=[SMEM] + [VMEM] * 3,
        out_specs=VMEM,
        out_shape=jax.ShapeDtypeStruct((copies, 8, 128), F32),
        scratch_shapes=[pltpu.VMEM((k, k), F32)],
        compiler_params=room(MIDDLE),
    )(core_id, inv, own, other)


def join_kernel(core_id, own, other, out):
    n, rows, _ = own.shape
    first = core_id[0] == 0
    half = rows * 128
    for b in range(0, n, 8):
        x = jnp.swapaxes(own[b : b + 8], 0, 1)
        y = jnp.swapaxes(other[b : b + 8], 0, 1)
        for r in range(rows):
            at = r * 128
            out[b : b + 8, at : at + 128] = jnp.where(first, x[r], y[r])
            out[b : b + 8, half + at : half + at + 128] = jnp.where(first, y[r], x[r])


def joined(core_id, own, other):
    n, rows, _ = own.shape
    return pl.pallas_call(
        join_kernel,
        in_specs=[SMEM, VMEM, VMEM],
        out_specs=VMEM,
        out_shape=jax.ShapeDtypeStruct((n, 2 * rows * 128), F32),
        compiler_params=room(MIDDLE),
    )(core_id, own, other)


def pair(x):
    return lax.ppermute(x, "c", [(0, 1), (1, 0)])


def exchange(x, axes):
    return lax.all_to_all(x, axes, 0, 0)


def of_four(x, axes):
    return [x] + [lax.ppermute(x, axes, [(i, i ^ s) for i in range(4)]) for s in (1, 2, 3)]


def spread(x, axes):
    n = math.prod(lax.axis_size(a) for a in axes)
    return exchange(jnp.broadcast_to(x, (n,) + x.shape), axes)


def both(x, axis):
    other = pair(x)
    first = lax.axis_index("c") == 0
    return jnp.where(
        first, jnp.concatenate([x, other], axis), jnp.concatenate([other, x], axis)
    )


def on_device(field, init_y, init_t, sketch_x, sketch_y, sketch_t):
    rows_x, rows_y, rows_t = field.shape
    r3 = init_t.shape[1]
    r1 = sketch_x.shape[1]
    scale_x = math.sqrt(rows_x * lax.axis_size(("y", "h")))
    scale_y = math.sqrt(rows_y * lax.axis_size("z"))
    scale_t = math.sqrt(rows_t * lax.axis_size(("l", "c")))
    core_id = lax.axis_index("c").astype(jnp.int32).reshape(1)

    w, zx = first(field, init_t.T, init_y.T, sketch_x.T, 8)
    zx = exchange(zx, ("z", "l"))
    zx, gx = gram_of(8, zx, pair(zx))
    sk_y = prepared_y(sketch_y.T, r3)
    qx, factor_x, mine, other = second(
        core_id, exchange(gx, ("y", "h")), zx, sk_y, w, scale_x, r3
    )
    wx = contract_x(qx, field)
    zy = spread(mine + pair(other), ("y", "h", "l")).sum(0)
    zy, wx = lax.optimization_barrier((zy, wx))
    zy, gy = gram_of(1, both(zy, 0)[None])
    factor_y, part, zt = third(of_four(gy[0], "z"), zy, sketch_t.T, wx, scale_y, 32, r1)
    zt, gt, core = core_terms(exchange(zt, ("y", "h", "z")), part, r1)
    factor_t, inv_t = last_factor(of_four(gt, ("l", "c")), zt, scale_t)
    chips = ("y", "h", "z", "l")
    piece, inv_t = lax.optimization_barrier((exchange(core, chips).sum(0), inv_t))
    core = exchange(scaled(core_id, inv_t, piece, pair(piece), r1), chips)
    core = joined(core_id, core, pair(core))
    return factor_x.T, factor_y.T, factor_t.T, core


def solution(mesh):
    fine = Mesh(mesh.devices.reshape(4, 2, 4, 2, 2), ("y", "h", "z", "l", "c"))
    gx, gy, ta = ("y", "h"), "z", ("l", "c")
    in_specs = (P(gx, gy, ta), P(gy, None), P(ta, None), P(), P(), P())
    out_specs = (P(gx, None), P(gy, None), P(ta, None), P())
    return jax.shard_map(
        on_device, mesh=fine, in_specs=in_specs, out_specs=out_specs, check_vma=False
    )
```

```python
import math

import jax
import jax.numpy as jnp
from jax import lax
from jax.experimental import pallas as pl
from jax.experimental.pallas import tpu as pltpu
from jax.sharding import Mesh, PartitionSpec as P

HIGH = lax.Precision.HIGHEST
F32 = jnp.float32
BF16 = jnp.bfloat16
VMEM = pl.BlockSpec(memory_space=pltpu.VMEM)
HBM = pl.BlockSpec(memory_space=pltpu.HBM)
SMEM = pl.BlockSpec(memory_space=pltpu.SMEM)
MOST = 58 * 1024 * 1024
BIG = 49 * 1024 * 1024
AHEAD = 4
MIDDLE = 4 * 1024 * 1024


def room(size):
    return pltpu.CompilerParams(vmem_limit_bytes=size)


def split(x):
    hi = x.astype(BF16)
    return hi, (x - hi.astype(F32)).astype(BF16)


def twice(x):
    hi, lo = split(x)
    return jnp.concatenate([jnp.concatenate([hi, hi], 1), jnp.concatenate([lo, lo], 1)], 0)


def dot(a, b, da=1, db=0, precision=None):
    return lax.dot_general(
        a, b, (((da,), (db,)), ((), ())), precision=precision, preferred_element_type=F32
    )


def tree_sum(parts):
    parts = list(parts)
    while len(parts) > 1:
        even = [parts[i] + parts[i + 1] for i in range(0, len(parts) - 1, 2)]
        parts = even + parts[len(even) * 2 :]
    return parts[0]


def cholesky_inverse(g):
    n = g.shape[0]
    nb = n // 8
    lane = lax.broadcasted_iota(jnp.int32, (8, 128), 1)
    sub = lax.broadcasted_iota(jnp.int32, (8, 128), 0)
    blocks = []
    for k in range(nb):
        eye = (lane - n == sub + 8 * k).astype(F32)
        wide = jnp.concatenate([g[8 * k : 8 * k + 8, :], jnp.zeros((8, 128 - n), F32)], 1)
        blocks.append(jnp.where(lane < n, wide, eye))
    out = []
    for kb in range(nb):
        rows = blocks[kb]
        cols = [
            jnp.broadcast_to(rows[:, 8 * kb + j : 8 * kb + j + 1], (8, 128)) for j in range(8)
        ]
        done = rows
        for p in range(8):
            inv = 1.0 / cols[p][p : p + 1, :]
            at = sub == p
            done = jnp.where(at, rows * lax.rsqrt(cols[p]), done)
            pivot = rows[p : p + 1, :] * inv
            rows = jnp.where(at, pivot, rows - cols[p] * pivot)
            for j in range(p + 1, 8):
                c = cols[j][p : p + 1, :] * inv
                cols[j] = jnp.where(at, c, cols[j] - cols[p] * c)
        out.append(done)
        for m in range(kb + 1, nb):
            b = blocks[m]
            blocks[m] = b - tree_sum(
                [b[:, 8 * kb + j : 8 * kb + j + 1] * rows[j : j + 1, :] for j in range(8)]
            )
    return jnp.concatenate(out, 0)[:, n : 2 * n]


def fold(g):
    return jnp.concatenate([g[:32], g[32:]], 1)


def unfold(g):
    return jnp.concatenate([g[:, :64], g[:, 64:]], 0)


def first_kernel(
    field, init_t, init_y, sketch, w, z, held, pair_w, in_t, in_y, in_s, lhs, unfolded, sems, out_sems
):
    nx, ny, nt = held.shape
    r3, r2, k = init_t.shape[0], init_y.shape[0], sketch.shape[0]
    chunks = out_sems.shape[0]
    rows = nx // chunks

    def copy(i):
        s = pl.ds(i * rows, rows)
        return pltpu.make_async_copy(field.at[s], held.at[s], sems.at[i])

    def copy_out(i, part):
        s = pl.ds(pl.multiple_of(i * rows + part * nx, 16), rows)
        return pltpu.make_async_copy(
            pair_w.at[:, s, :], w.at[pl.ds(0, r3), s, :], out_sems.at[i, part]
        )

    small = [
        pltpu.make_async_copy(init_t, in_t, sems.at[chunks]),
        pltpu.make_async_copy(init_y, in_y, sems.at[chunks + 1]),
        pltpu.make_async_copy(sketch, in_s, sems.at[chunks + 2]),
    ]
    for c in small:
        c.start()
    for i in range(AHEAD):
        copy(i).start()
    small[0].wait()
    lhs[...] = twice(in_t[...])

    def chunk(i, _):
        copy(i).wait()

        @pl.when(i + AHEAD < chunks)
        def _():
            copy(i + AHEAD).start()

        groups = []
        for x8 in range(0, rows, 8):
            outs = []
            for x in range(8):
                hi, lo = split(held[i * rows + x8 + x])
                o = dot(lhs[...], jnp.concatenate([hi, lo], 1), 1, 1)
                outs.append(o[:r3] + o[r3:])
            groups.append(jnp.swapaxes(jnp.stack(outs, 0), 0, 1))
        hi, lo = split(jnp.concatenate(groups, 1))
        at = pl.multiple_of(i * rows, 16)
        pair_w[:, pl.ds(at, rows), :] = hi
        pair_w[:, pl.ds(pl.multiple_of(at + nx, 16), rows), :] = lo
        copy_out(i, 0).start()
        copy_out(i, 1).start()
        return 0

    lax.fori_loop(0, chunks, chunk, 0)
    small[1].wait()
    small[2].wait()
    hi, lo = split(in_y[...])
    left = jnp.concatenate([hi, lo], 0)
    for c8 in range(0, r3, 8):
        outs = []
        for c in range(c8, c8 + 8):
            o = dot(left, pair_w[c], 1, 1)
            outs.append((o[r2:, :nx] + o[:r2, nx:] + o[r2:, nx:]) + o[:r2, :nx])
        unfolded[:, c8 : c8 + 8, :] = jnp.swapaxes(jnp.stack(outs, 0), 0, 1)
    acc = None
    for a in range(0, r2, 8):
        hi, lo = split(unfolded[a : a + 8].reshape(8 * r3, nx))
        sh, sl = split(in_s[:, a * r3 : (a + 8) * r3])
        o = dot(jnp.concatenate([sh, sl], 0), jnp.concatenate([hi, lo], 1))
        acc = o if acc is None else acc + o
    total = (acc[k:, :nx] + acc[:k, nx:] + acc[k:, nx:]) + acc[:k, :nx]
    for i in range(z.shape[0]):
        z[i] = total
    for i in range(chunks):
        copy_out(i, 0).wait()
        copy_out(i, 1).wait()


def first(field, init_t, init_y, sketch, copies):
    nx, ny, nt = field.shape
    r3, r2, k = init_t.shape[0], init_y.shape[0], sketch.shape[0]
    return pl.pallas_call(
        first_kernel,
        in_specs=[HBM, HBM, HBM, HBM],
        out_specs=[HBM, VMEM],
        out_shape=[
            jax.ShapeDtypeStruct((4 * r3, 2 * nx, ny), BF16),
            jax.ShapeDtypeStruct((copies, k, nx), F32),
        ],
        scratch_shapes=[
            pltpu.VMEM((nx, ny, nt), F32),
            pltpu.VMEM((r3, 2 * nx, ny), BF16),
            pltpu.VMEM(init_t.shape, F32),
            pltpu.VMEM(init_y.shape, F32),
            pltpu.VMEM(sketch.shape, F32),
            pltpu.VMEM((2 * r3, 2 * nt), BF16),
            pltpu.VMEM((r2, r3, nx), F32),
            pltpu.SemaphoreType.DMA((11,)),
            pltpu.SemaphoreType.DMA((8, 2)),
        ],
        compiler_params=room(MOST),
        cost_estimate=pl.CostEstimate(
            flops=8 * nx * ny * nt * r3, bytes_accessed=nx * ny * nt * 4, transcendentals=0
        ),
    )(field, init_t, init_y, sketch)


def gram_kernel(*refs):
    *parts, z, gram = refs
    total = sum(tree_sum([p[i] for i in range(p.shape[0])]) for p in parts)
    z[...] = total
    g = fold(dot(total, total, 1, 1, HIGH))
    for i in range(gram.shape[0]):
        gram[i] = g


def gram_of(copies, *parts):
    k, n = parts[0].shape[1:]
    return pl.pallas_call(
        gram_kernel,
        in_specs=[VMEM] * len(parts),
        out_specs=[VMEM, VMEM],
        out_shape=[
            jax.ShapeDtypeStruct((k, n), F32),
            jax.ShapeDtypeStruct((copies, k * k // 128, 128), F32),
        ],
        compiler_params=room(MIDDLE),
    )(*parts)


def sketch_y_kernel(sketch, out, turned):
    k = sketch.shape[0]
    r3 = out.shape[0] // k
    r1 = sketch.shape[1] // r3
    for i in range(0, r1 * r3, 128):
        turned[i : i + 128, :] = sketch[:, i : i + 128].T
    for c in range(r3):
        hi, lo = split(turned[pl.ds(c, r1, stride=r3), :].T)
        out[c * k : (c + 1) * k, :] = jnp.concatenate([hi, lo, hi, lo], 1)


def prepared_y(sketch, r3):
    k, n = sketch.shape
    return pl.pallas_call(
        sketch_y_kernel,
        in_specs=[VMEM],
        out_specs=VMEM,
        out_shape=jax.ShapeDtypeStruct((r3 * k, 4 * n // r3), BF16),
        scratch_shapes=[pltpu.VMEM((n, k), F32)],
        compiler_params=room(MIDDLE),
        cost_estimate=pl.CostEstimate(flops=10**7, bytes_accessed=2 * 10**6, transcendentals=0),
    )(sketch)


def project_kernel(z, w, u, pair_w, sems):
    r3 = pair_w.shape[0]
    r1 = z.shape[0]
    each = r3 // sems.shape[0]

    def copy(i):
        s = pl.ds(i * each, each)
        return pltpu.make_async_copy(w.at[s], pair_w.at[s], sems.at[i])

    def start(i, _):
        copy(i).start()
        return 0

    lax.fori_loop(0, r3 // each, start, 0)
    lhs = twice(z[...])
    for c in range(r3):
        if c % each == 0:
            copy(c // each).wait()
        o = dot(lhs, pair_w[c])
        hi, lo = split(o[r1:] + o[:r1])
        u[c * r1 : (c + 1) * r1, :] = jnp.concatenate([hi, lo], 1)


def project(z, w, r3):
    r1, nx = z.shape
    ny = w.shape[2]
    return pl.pallas_call(
        project_kernel,
        in_specs=[VMEM, HBM],
        out_specs=VMEM,
        out_shape=jax.ShapeDtypeStruct((r3 * r1, 2 * ny), BF16),
        scratch_shapes=[
            pltpu.VMEM((r3, 2 * nx, ny), BF16),
            pltpu.SemaphoreType.DMA((2,)),
        ],
        compiler_params=room(BIG),
        cost_estimate=pl.CostEstimate(flops=10**9, bytes_accessed=6 * 10**6, transcendentals=0),
    )(z, w)


def second_kernel(scale, core_id, grams, z, sk, u, q, factor, mine, other):
    g = unfold(tree_sum([grams[i] for i in range(grams.shape[0])]))
    inv = cholesky_inverse(g)
    hi, lo = split(inv)
    mixed = dot(sk[...], jnp.concatenate([hi, hi, lo, lo], 0))
    half = mine.shape[0]
    k = 2 * half
    ny = mine.shape[1]
    r1 = z.shape[0]
    group = 4
    acc = None
    for c in range(0, mixed.shape[0] // k, group):
        left = jnp.concatenate([mixed[(c + i) * k : (c + i + 1) * k] for i in range(group)], 1)
        hi, lo = split(left)
        o = dot(jnp.concatenate([hi, lo], 0), u[c * r1 : (c + group) * r1, :])
        acc = o if acc is None else acc + o
    zy = (acc[k:, :ny] + acc[:k, ny:] + acc[k:, ny:]) + acc[:k, :ny]
    first = core_id[0] == 0
    mine[...] = jnp.where(first, zy[:half], zy[half:])
    other[...] = jnp.where(first, zy[half:], zy[:half])
    qv = dot(inv, z[...], 1, 0, HIGH)
    q[...] = qv
    factor[...] = qv * scale


def second(core_id, grams, z, sk, u, scale, r3):
    r1, nx = z.shape
    half = jax.ShapeDtypeStruct((sk.shape[0] // r3 // 2, u.shape[1] // 2), F32)
    return pl.pallas_call(
        lambda *a: second_kernel(scale, *a),
        in_specs=[SMEM] + [VMEM] * 4,
        out_specs=[VMEM] * 4,
        out_shape=[
            jax.ShapeDtypeStruct((r1, nx), F32),
            jax.ShapeDtypeStruct((r1, nx), F32),
            half,
            half,
        ],
        compiler_params=room(8 * 1024 * 1024),
    )(core_id, grams, z, sk, u)


def contract_x_kernel(q, field, wx, held, out, lhs, sems, out_sems):
    nx, ny, nt = held.shape
    r1 = q.shape[0]
    chunks = sems.shape[0]
    rows = ny // chunks

    def copy(i):
        s = pl.ds(pl.multiple_of(i * rows, 8), rows)
        return pltpu.make_async_copy(field.at[:, s, :], held.at[:, s, :], sems.at[i])

    def copy_out(i):
        s = pl.ds(pl.multiple_of(i * rows, 8), rows)
        return pltpu.make_async_copy(
            out.at[:, s, :], wx.at[pl.ds(0, r1), s, :], out_sems.at[i]
        )

    for i in range(AHEAD):
        copy(i).start()
    lhs[...] = twice(q[...])

    def chunk(i, _):
        copy(i).wait()

        @pl.when(i + AHEAD < chunks)
        def _():
            copy(i + AHEAD).start()

        for y8 in range(0, rows, 8):
            at = pl.multiple_of(i * rows + y8, 8)
            f = jnp.swapaxes(held[:, pl.ds(at, 8), :], 0, 1)
            outs = []
            for y in range(0, 8, 2):
                h0, l0 = split(f[y])
                h1, l1 = split(f[y + 1])
                rhs = jnp.concatenate(
                    [jnp.concatenate([h0, h1], 1), jnp.concatenate([l0, l1], 1)], 0
                )
                o = dot(lhs[...], rhs)
                o = o[r1:] + o[:r1]
                outs += [o[:, :nt], o[:, nt:]]
            out[:, pl.ds(at, 8), :] = jnp.swapaxes(jnp.stack(outs, 0), 0, 1)
        copy_out(i).start()
        return 0

    lax.fori_loop(0, chunks, chunk, 0)
    for i in range(chunks):
        copy_out(i).wait()


def contract_x(q, field):
    nx, ny, nt = field.shape
    r1 = q.shape[0]
    chunks = ny // 32
    return pl.pallas_call(
        contract_x_kernel,
        in_specs=[VMEM, HBM],
        out_specs=HBM,
        out_shape=jax.ShapeDtypeStruct((2 * r1, ny, nt), F32),
        scratch_shapes=[
            pltpu.VMEM((nx, ny, nt), F32),
            pltpu.VMEM((r1, ny, nt), F32),
            pltpu.VMEM((2 * r1, 2 * nx), BF16),
            pltpu.SemaphoreType.DMA((chunks,)),
            pltpu.SemaphoreType.DMA((chunks,)),
        ],
        compiler_params=room(BIG),
        cost_estimate=pl.CostEstimate(
            flops=8 * nx * ny * nt * r1, bytes_accessed=nx * ny * nt * 6, transcendentals=0
        ),
    )(q, field)


def third_kernel(scale, g0, g1, g2, g3, z, sketch, wa, factor, part, zt, wx, sems):
    r1, ny, nt = wx.shape
    r2 = z.shape[0]
    chunks = sems.shape[0]
    rows = r1 // chunks

    def copy(i):
        s = pl.ds(i * rows, rows)
        return pltpu.make_async_copy(wa.at[s], wx.at[s], sems.at[i])

    def start(i, _):
        copy(i).start()
        return 0

    lax.fori_loop(0, chunks, start, 0)
    g = unfold((g0[...] + g1[...]) + (g2[...] + g3[...]))
    qv = dot(cholesky_inverse(g), z[...], 1, 0, HIGH)
    factor[...] = qv * scale
    hi, lo = split(qv)
    lhs = jnp.concatenate([hi, lo], 0)
    k = sketch.shape[0]
    group = 4

    def step(i, acc):
        copy(i).wait()
        for b in range(rows):
            hi, lo = split(wx[i * rows + b])
            o = dot(lhs, jnp.concatenate([hi, lo], 1))
            o = (o[r2:, :nt] + o[:r2, nt:] + o[r2:, nt:]) + o[:r2, :nt]
            hi, lo = split(o)
            at = pl.multiple_of((i * rows + b) * r2, r2)
            part[pl.ds(at, r2), :] = jnp.concatenate([hi, lo], 1)
        for b in range(0, rows, group):
            n = group * r2
            s = pl.ds(pl.multiple_of((i * rows + b) * r2, n), n)
            hi, lo = split(sketch[:, s])
            acc = acc + dot(jnp.concatenate([hi, lo], 0), part[s, :])
        return acc

    acc = jnp.zeros((2 * k, 2 * nt), F32)
    for i in range(chunks):
        acc = step(i, acc)
    total = (acc[k:, :nt] + acc[:k, nt:] + acc[k:, nt:]) + acc[:k, :nt]
    for i in range(zt.shape[0]):
        zt[i] = total


def third(grams, z, sketch, wa, scale, copies, r1):
    r2, ny = z.shape
    nt = wa.shape[2]
    k = sketch.shape[0]
    return pl.pallas_call(
        lambda *a: third_kernel(scale, *a),
        in_specs=[VMEM] * 6 + [HBM],
        out_specs=[VMEM] * 3,
        out_shape=[
            jax.ShapeDtypeStruct((r2, ny), F32),
            jax.ShapeDtypeStruct((r1 * r2, 2 * nt), BF16),
            jax.ShapeDtypeStruct((copies, k, nt), F32),
        ],
        scratch_shapes=[pltpu.VMEM((r1, ny, nt), F32), pltpu.SemaphoreType.DMA((2,))],
        compiler_params=room(BIG),
    )(*grams, z, sketch, wa)


def core_kernel(parts, part, z, gram, out):
    total = tree_sum([parts[i] for i in range(parts.shape[0])])
    z[...] = total
    gram[...] = dot(total, total, 1, 1, HIGH)
    k = total.shape[0]
    lhs = twice(total)
    group = lax.broadcasted_iota(jnp.int32, (8, 128), 1) // 32
    for i in range(part.shape[0] // 256):
        o = dot(lhs, part[i * 256 : (i + 1) * 256, :], 1, 1)
        o = o[k:] + o[:k]
        for j in range(2):
            v = [o[8 * g : 8 * g + 8, 128 * j : 128 * j + 128] for g in range(4)]
            for s in range(4):
                t = None
                for g in range(4):
                    shift = (g - s) * 32 % 128
                    u = pltpu.roll(v[g], shift, 1) if shift else v[g]
                    t = u if t is None else jnp.where(group == g, u, t)
                at = i * 4 + j * 2 + s // 2
                out[at, 8 * (s % 2) : 8 * (s % 2) + 8, :] = t


def core_terms(parts, part, r1):
    k, nt = parts.shape[1:]
    return pl.pallas_call(
        core_kernel,
        in_specs=[VMEM, VMEM],
        out_specs=[VMEM] * 3,
        out_shape=[
            jax.ShapeDtypeStruct((k, nt), F32),
            jax.ShapeDtypeStruct((k, k), F32),
            jax.ShapeDtypeStruct((r1, 16, 128), F32),
        ],
        compiler_params=room(MIDDLE),
    )(parts, part)


def inverse_kernel(scale, g0, g1, g2, g3, z, factor, inv):
    inv[...] = cholesky_inverse((g0[...] + g1[...]) + (g2[...] + g3[...]))
    factor[...] = dot(inv[...], z[...], 1, 0, HIGH) * scale


def last_factor(grams, z, scale):
    k, nt = z.shape
    return pl.pallas_call(
        lambda *a: inverse_kernel(scale, *a),
        in_specs=[VMEM] * 5,
        out_specs=[VMEM] * 2,
        out_shape=[jax.ShapeDtypeStruct((k, nt), F32), jax.ShapeDtypeStruct((k, k), F32)],
        compiler_params=room(MIDDLE),
        cost_estimate=pl.CostEstimate(flops=10**7, bytes_accessed=2 * 10**6, transcendentals=0),
    )(*grams, z)


def scale_kernel(core_id, inv, own, other, out, held):
    piece = own[...] + other[...]
    piece = jnp.where(core_id[0] == 0, piece[:8], piece[8:])
    x = jnp.concatenate([piece[:, 32 * g : 32 * g + 32] for g in range(4)], 0)
    held[...] = dot(x, inv[...], 0, 1, HIGH)
    row = jnp.concatenate([held[pl.ds(s, 8, stride=4), :] for s in range(4)], 1)
    for i in range(out.shape[0]):
        out[i] = row


def scaled(core_id, inv, own, other, copies):
    k = inv.shape[0]
    return pl.pallas_call(
        scale_kernel,
        in_specs=[SMEM] + [VMEM] * 3,
        out_specs=VMEM,
        out_shape=jax.ShapeDtypeStruct((copies, 8, 128), F32),
        scratch_shapes=[pltpu.VMEM((k, k), F32)],
        compiler_params=room(MIDDLE),
    )(core_id, inv, own, other)


def join_kernel(core_id, own, other, out):
    n, rows, _ = own.shape
    first = core_id[0] == 0
    half = rows * 128
    for b in range(0, n, 8):
        x = jnp.swapaxes(own[b : b + 8], 0, 1)
        y = jnp.swapaxes(other[b : b + 8], 0, 1)
        for r in range(rows):
            at = r * 128
            out[b : b + 8, at : at + 128] = jnp.where(first, x[r], y[r])
            out[b : b + 8, half + at : half + at + 128] = jnp.where(first, y[r], x[r])


def joined(core_id, own, other):
    n, rows, _ = own.shape
    return pl.pallas_call(
        join_kernel,
        in_specs=[SMEM, VMEM, VMEM],
        out_specs=VMEM,
        out_shape=jax.ShapeDtypeStruct((n, 2 * rows * 128), F32),
        compiler_params=room(MIDDLE),
    )(core_id, own, other)


def pair(x):
    return lax.ppermute(x, "c", [(0, 1), (1, 0)])


def exchange(x, axes):
    return lax.all_to_all(x, axes, 0, 0)


def of_four(x, axes):
    others = [lax.ppermute(x, axes, [(i, i ^ s) for i in range(4)]) for s in (3, 2, 1)]
    return [x] + others[::-1]


def spread(x, axes):
    n = math.prod(lax.axis_size(a) for a in axes)
    return exchange(jnp.broadcast_to(x, (n,) + x.shape), axes)


def both(x, axis):
    other = pair(x)
    first = lax.axis_index("c") == 0
    return jnp.where(
        first, jnp.concatenate([x, other], axis), jnp.concatenate([other, x], axis)
    )


def on_device(field, init_y, init_t, sketch_x, sketch_y, sketch_t):
    rows_x, rows_y, rows_t = field.shape
    r3 = init_t.shape[1]
    r1 = sketch_x.shape[1]
    scale_x = math.sqrt(rows_x * lax.axis_size(("y", "h")))
    scale_y = math.sqrt(rows_y * lax.axis_size("z"))
    scale_t = math.sqrt(rows_t * lax.axis_size(("l", "c")))
    core_id = lax.axis_index("c").astype(jnp.int32).reshape(1)

    w, zx = first(field, init_t.T, init_y.T, sketch_x.T, 8)
    zx = exchange(zx, ("z", "l"))
    zx, gx = gram_of(8, zx, pair(zx))
    sk_y = prepared_y(sketch_y.T, r3)
    u = project(zx, w, r3)
    gx, u = lax.optimization_barrier((exchange(gx, ("y", "h")), u))
    qx, factor_x, mine, other = second(core_id, gx, zx, sk_y, u, scale_x, r3)
    wx = contract_x(qx, field)
    zy = spread(mine + pair(other), ("y", "h", "l")).sum(0)
    zy, wx = lax.optimization_barrier((zy, wx))
    zy, gy = gram_of(1, both(zy, 0)[None])
    factor_y, part, zt = third(of_four(gy[0], "z"), zy, sketch_t.T, wx, scale_y, 32, r1)
    zt, gt, core = core_terms(exchange(zt, ("y", "h", "z")), part, r1)
    chips = ("y", "h", "z", "l")
    piece = exchange(core, chips).sum(0)
    piece, gt = lax.optimization_barrier((piece, of_four(gt, ("l", "c"))))
    factor_t, inv_t = last_factor(gt, zt, scale_t)
    core = exchange(scaled(core_id, inv_t, piece, pair(piece), r1), chips)
    core = joined(core_id, core, pair(core))
    return factor_x.T, factor_y.T, factor_t.T, core


def solution(mesh):
    fine = Mesh(mesh.devices.reshape(4, 2, 4, 2, 2), ("y", "h", "z", "l", "c"))
    gx, gy, ta = ("y", "h"), "z", ("l", "c")
    in_specs = (P(gx, gy, ta), P(gy, None), P(ta, None), P(), P(), P())
    out_specs = (P(gx, None), P(gy, None), P(ta, None), P())
    return jax.shard_map(
        on_device, mesh=fine, in_specs=in_specs, out_specs=out_specs, check_vma=False
    )
```

```python
import math

import jax
import jax.numpy as jnp
from jax import lax
from jax.experimental import pallas as pl
from jax.experimental.pallas import tpu as pltpu
from jax.sharding import Mesh, PartitionSpec as P

HIGH = lax.Precision.HIGHEST
F32 = jnp.float32
BF16 = jnp.bfloat16
VMEM = pl.BlockSpec(memory_space=pltpu.VMEM)
HBM = pl.BlockSpec(memory_space=pltpu.HBM)
SMEM = pl.BlockSpec(memory_space=pltpu.SMEM)
MOST = 58 * 1024 * 1024
BIG = 49 * 1024 * 1024
AHEAD = 4
MIDDLE = 4 * 1024 * 1024


def room(size):
    return pltpu.CompilerParams(vmem_limit_bytes=size)


def split(x):
    hi = x.astype(BF16)
    return hi, (x - hi.astype(F32)).astype(BF16)


def twice(x):
    hi, lo = split(x)
    return jnp.concatenate([jnp.concatenate([hi, hi], 1), jnp.concatenate([lo, lo], 1)], 0)


def dot(a, b, da=1, db=0, precision=None):
    return lax.dot_general(
        a, b, (((da,), (db,)), ((), ())), precision=precision, preferred_element_type=F32
    )


def tree_sum(parts):
    parts = list(parts)
    while len(parts) > 1:
        even = [parts[i] + parts[i + 1] for i in range(0, len(parts) - 1, 2)]
        parts = even + parts[len(even) * 2 :]
    return parts[0]


def cholesky_inverse(g):
    n = g.shape[0]
    nb = n // 8
    lane = lax.broadcasted_iota(jnp.int32, (8, 128), 1)
    sub = lax.broadcasted_iota(jnp.int32, (8, 128), 0)
    blocks = []
    for k in range(nb):
        eye = (lane - n == sub + 8 * k).astype(F32)
        wide = jnp.concatenate([g[8 * k : 8 * k + 8, :], jnp.zeros((8, 128 - n), F32)], 1)
        blocks.append(jnp.where(lane < n, wide, eye))
    out = []
    for kb in range(nb):
        rows = blocks[kb]
        cols = [
            jnp.broadcast_to(rows[:, 8 * kb + j : 8 * kb + j + 1], (8, 128)) for j in range(8)
        ]
        done = rows
        for p in range(8):
            inv = 1.0 / cols[p][p : p + 1, :]
            at = sub == p
            done = jnp.where(at, rows * lax.rsqrt(cols[p]), done)
            pivot = rows[p : p + 1, :] * inv
            rows = jnp.where(at, pivot, rows - cols[p] * pivot)
            for j in range(p + 1, 8):
                c = cols[j][p : p + 1, :] * inv
                cols[j] = jnp.where(at, c, cols[j] - cols[p] * c)
        out.append(done)
        for m in range(kb + 1, nb):
            b = blocks[m]
            blocks[m] = b - tree_sum(
                [b[:, 8 * kb + j : 8 * kb + j + 1] * rows[j : j + 1, :] for j in range(8)]
            )
    return jnp.concatenate(out, 0)[:, n : 2 * n]


def fold(g):
    return jnp.concatenate([g[:32], g[32:]], 1)


def unfold(g):
    return jnp.concatenate([g[:, :64], g[:, 64:]], 0)


def first_kernel(
    field, init_t, init_y, sketch, w, z, held, pair_w, in_t, in_y, in_s, lhs, unfolded, sems, out_sems
):
    nx, ny, nt = held.shape
    r3, r2, k = init_t.shape[0], init_y.shape[0], sketch.shape[0]
    chunks = out_sems.shape[0]
    rows = nx // chunks

    def copy(i):
        s = pl.ds(i * rows, rows)
        return pltpu.make_async_copy(field.at[s], held.at[s], sems.at[i])

    def copy_out(i, part):
        s = pl.ds(pl.multiple_of(i * rows + part * nx, 16), rows)
        return pltpu.make_async_copy(
            pair_w.at[:, s, :], w.at[pl.ds(0, r3), s, :], out_sems.at[i, part]
        )

    small = [
        pltpu.make_async_copy(init_t, in_t, sems.at[chunks]),
        pltpu.make_async_copy(init_y, in_y, sems.at[chunks + 1]),
        pltpu.make_async_copy(sketch, in_s, sems.at[chunks + 2]),
    ]
    for c in small:
        c.start()
    for i in range(AHEAD):
        copy(i).start()
    small[0].wait()
    lhs[...] = twice(in_t[...])

    def chunk(i, _):
        copy(i).wait()

        @pl.when(i + AHEAD < chunks)
        def _():
            copy(i + AHEAD).start()

        groups = []
        for x8 in range(0, rows, 8):
            outs = []
            for x in range(8):
                hi, lo = split(held[i * rows + x8 + x])
                o = dot(lhs[...], jnp.concatenate([hi, lo], 1), 1, 1)
                outs.append(o[:r3] + o[r3:])
            groups.append(jnp.swapaxes(jnp.stack(outs, 0), 0, 1))
        hi, lo = split(jnp.concatenate(groups, 1))
        at = pl.multiple_of(i * rows, 16)
        pair_w[:, pl.ds(at, rows), :] = hi
        pair_w[:, pl.ds(pl.multiple_of(at + nx, 16), rows), :] = lo
        copy_out(i, 0).start()
        copy_out(i, 1).start()
        return 0

    lax.fori_loop(0, chunks, chunk, 0)
    small[1].wait()
    small[2].wait()
    hi, lo = split(in_y[...])
    left = jnp.concatenate([hi, lo], 0)
    for c8 in range(0, r3, 8):
        outs = []
        for c in range(c8, c8 + 8):
            o = dot(left, pair_w[c], 1, 1)
            outs.append((o[r2:, :nx] + o[:r2, nx:] + o[r2:, nx:]) + o[:r2, :nx])
        unfolded[:, c8 : c8 + 8, :] = jnp.swapaxes(jnp.stack(outs, 0), 0, 1)
    acc = None
    for a in range(0, r2, 8):
        hi, lo = split(unfolded[a : a + 8].reshape(8 * r3, nx))
        sh, sl = split(in_s[:, a * r3 : (a + 8) * r3])
        o = dot(jnp.concatenate([sh, sl], 0), jnp.concatenate([hi, lo], 1))
        acc = o if acc is None else acc + o
    total = (acc[k:, :nx] + acc[:k, nx:] + acc[k:, nx:]) + acc[:k, :nx]
    for i in range(z.shape[0]):
        z[i] = total
    for i in range(chunks):
        copy_out(i, 0).wait()
        copy_out(i, 1).wait()


def first(field, init_t, init_y, sketch, copies):
    nx, ny, nt = field.shape
    r3, r2, k = init_t.shape[0], init_y.shape[0], sketch.shape[0]
    return pl.pallas_call(
        first_kernel,
        in_specs=[HBM, HBM, HBM, HBM],
        out_specs=[HBM, VMEM],
        out_shape=[
            jax.ShapeDtypeStruct((4 * r3, 2 * nx, ny), BF16),
            jax.ShapeDtypeStruct((copies, k, nx), F32),
        ],
        scratch_shapes=[
            pltpu.VMEM((nx, ny, nt), F32),
            pltpu.VMEM((r3, 2 * nx, ny), BF16),
            pltpu.VMEM(init_t.shape, F32),
            pltpu.VMEM(init_y.shape, F32),
            pltpu.VMEM(sketch.shape, F32),
            pltpu.VMEM((2 * r3, 2 * nt), BF16),
            pltpu.VMEM((r2, r3, nx), F32),
            pltpu.SemaphoreType.DMA((11,)),
            pltpu.SemaphoreType.DMA((8, 2)),
        ],
        compiler_params=room(MOST),
        cost_estimate=pl.CostEstimate(
            flops=8 * nx * ny * nt * r3, bytes_accessed=nx * ny * nt * 4, transcendentals=0
        ),
    )(field, init_t, init_y, sketch)


def gram_kernel(*refs):
    *parts, z, gram = refs
    total = sum(tree_sum([p[i] for i in range(p.shape[0])]) for p in parts)
    z[...] = total
    g = fold(dot(total, total, 1, 1, HIGH))
    for i in range(gram.shape[0]):
        gram[i] = g


def gram_of(copies, *parts):
    k, n = parts[0].shape[1:]
    return pl.pallas_call(
        gram_kernel,
        in_specs=[VMEM] * len(parts),
        out_specs=[VMEM, VMEM],
        out_shape=[
            jax.ShapeDtypeStruct((k, n), F32),
            jax.ShapeDtypeStruct((copies, k * k // 128, 128), F32),
        ],
        compiler_params=room(MIDDLE),
    )(*parts)


def sketch_y_kernel(sketch, out, turned):
    k = sketch.shape[0]
    r3 = out.shape[0] // k
    r1 = sketch.shape[1] // r3
    for i in range(0, r1 * r3, 128):
        turned[i : i + 128, :] = sketch[:, i : i + 128].T
    for c in range(r3):
        hi, lo = split(turned[pl.ds(c, r1, stride=r3), :].T)
        out[c * k : (c + 1) * k, :] = jnp.concatenate([hi, lo, hi, lo], 1)


def prepared_y(sketch, r3):
    k, n = sketch.shape
    return pl.pallas_call(
        sketch_y_kernel,
        in_specs=[VMEM],
        out_specs=VMEM,
        out_shape=jax.ShapeDtypeStruct((r3 * k, 4 * n // r3), BF16),
        scratch_shapes=[pltpu.VMEM((n, k), F32)],
        compiler_params=room(MIDDLE),
        cost_estimate=pl.CostEstimate(flops=10**7, bytes_accessed=2 * 10**6, transcendentals=0),
    )(sketch)


def project_kernel(z, w, u, pair_w, sems):
    r3 = pair_w.shape[0]
    r1 = z.shape[0]
    each = r3 // sems.shape[0]

    def copy(i):
        s = pl.ds(i * each, each)
        return pltpu.make_async_copy(w.at[s], pair_w.at[s], sems.at[i])

    def start(i, _):
        copy(i).start()
        return 0

    lax.fori_loop(0, r3 // each, start, 0)
    lhs = twice(z[...])
    for c in range(r3):
        if c % each == 0:
            copy(c // each).wait()
        o = dot(lhs, pair_w[c])
        hi, lo = split(o[r1:] + o[:r1])
        u[c * r1 : (c + 1) * r1, :] = jnp.concatenate([hi, lo], 1)


def project(z, w, r3):
    r1, nx = z.shape
    ny = w.shape[2]
    return pl.pallas_call(
        project_kernel,
        in_specs=[VMEM, HBM],
        out_specs=VMEM,
        out_shape=jax.ShapeDtypeStruct((r3 * r1, 2 * ny), BF16),
        scratch_shapes=[
            pltpu.VMEM((r3, 2 * nx, ny), BF16),
            pltpu.SemaphoreType.DMA((2,)),
        ],
        compiler_params=room(BIG),
        cost_estimate=pl.CostEstimate(flops=10**9, bytes_accessed=6 * 10**6, transcendentals=0),
    )(z, w)


def second_kernel(scale, core_id, grams, z, sk, u, q, factor, mine, other):
    g = unfold(tree_sum([grams[i] for i in range(grams.shape[0])]))
    inv = cholesky_inverse(g)
    hi, lo = split(inv)
    mixed = dot(sk[...], jnp.concatenate([hi, hi, lo, lo], 0))
    half = mine.shape[0]
    k = 2 * half
    ny = mine.shape[1]
    r1 = z.shape[0]
    group = 4
    acc = None
    for c in range(0, mixed.shape[0] // k, group):
        left = jnp.concatenate([mixed[(c + i) * k : (c + i + 1) * k] for i in range(group)], 1)
        hi, lo = split(left)
        o = dot(jnp.concatenate([hi, lo], 0), u[c * r1 : (c + group) * r1, :])
        acc = o if acc is None else acc + o
    zy = (acc[k:, :ny] + acc[:k, ny:] + acc[k:, ny:]) + acc[:k, :ny]
    first = core_id[0] == 0
    mine[...] = jnp.where(first, zy[:half], zy[half:])
    other[...] = jnp.where(first, zy[half:], zy[:half])
    qv = dot(inv, z[...], 1, 0, HIGH)
    q[...] = qv
    factor[...] = qv * scale


def second(core_id, grams, z, sk, u, scale, r3):
    r1, nx = z.shape
    half = jax.ShapeDtypeStruct((sk.shape[0] // r3 // 2, u.shape[1] // 2), F32)
    return pl.pallas_call(
        lambda *a: second_kernel(scale, *a),
        in_specs=[SMEM] + [VMEM] * 4,
        out_specs=[VMEM] * 4,
        out_shape=[
            jax.ShapeDtypeStruct((r1, nx), F32),
            jax.ShapeDtypeStruct((r1, nx), F32),
            half,
            half,
        ],
        compiler_params=room(8 * 1024 * 1024),
    )(core_id, grams, z, sk, u)


def contract_x_kernel(q, field, wx, held, out, lhs, sems, out_sems):
    nx, ny, nt = held.shape
    r1 = q.shape[0]
    chunks = sems.shape[0]
    rows = ny // chunks

    def copy(i):
        s = pl.ds(pl.multiple_of(i * rows, 8), rows)
        return pltpu.make_async_copy(field.at[:, s, :], held.at[:, s, :], sems.at[i])

    def copy_out(i):
        s = pl.ds(pl.multiple_of(i * rows, 8), rows)
        return pltpu.make_async_copy(
            out.at[:, s, :], wx.at[pl.ds(0, r1), s, :], out_sems.at[i]
        )

    for i in range(AHEAD):
        copy(i).start()
    lhs[...] = twice(q[...])

    def chunk(i, _):
        copy(i).wait()

        @pl.when(i + AHEAD < chunks)
        def _():
            copy(i + AHEAD).start()

        for y8 in range(0, rows, 8):
            at = pl.multiple_of(i * rows + y8, 8)
            f = jnp.swapaxes(held[:, pl.ds(at, 8), :], 0, 1)
            outs = []
            for y in range(0, 8, 2):
                h0, l0 = split(f[y])
                h1, l1 = split(f[y + 1])
                rhs = jnp.concatenate(
                    [jnp.concatenate([h0, h1], 1), jnp.concatenate([l0, l1], 1)], 0
                )
                o = dot(lhs[...], rhs)
                o = o[r1:] + o[:r1]
                outs += [o[:, :nt], o[:, nt:]]
            out[:, pl.ds(at, 8), :] = jnp.swapaxes(jnp.stack(outs, 0), 0, 1)
        copy_out(i).start()
        return 0

    lax.fori_loop(0, chunks, chunk, 0)
    for i in range(chunks):
        copy_out(i).wait()


def contract_x(q, field):
    nx, ny, nt = field.shape
    r1 = q.shape[0]
    chunks = ny // 32
    return pl.pallas_call(
        contract_x_kernel,
        in_specs=[VMEM, HBM],
        out_specs=HBM,
        out_shape=jax.ShapeDtypeStruct((2 * r1, ny, nt), F32),
        scratch_shapes=[
            pltpu.VMEM((nx, ny, nt), F32),
            pltpu.VMEM((r1, ny, nt), F32),
            pltpu.VMEM((2 * r1, 2 * nx), BF16),
            pltpu.SemaphoreType.DMA((chunks,)),
            pltpu.SemaphoreType.DMA((chunks,)),
        ],
        compiler_params=room(BIG),
        cost_estimate=pl.CostEstimate(
            flops=8 * nx * ny * nt * r1, bytes_accessed=nx * ny * nt * 6, transcendentals=0
        ),
    )(q, field)


def third_kernel(scale, g0, g1, g2, g3, z, sketch, wa, factor, part, zt, wx, sems):
    r1, ny, nt = wx.shape
    r2 = z.shape[0]
    chunks = sems.shape[0]
    rows = r1 // chunks

    def copy(i):
        s = pl.ds(i * rows, rows)
        return pltpu.make_async_copy(wa.at[s], wx.at[s], sems.at[i])

    def start(i, _):
        copy(i).start()
        return 0

    lax.fori_loop(0, chunks, start, 0)
    g = unfold((g0[...] + g1[...]) + (g2[...] + g3[...]))
    qv = dot(cholesky_inverse(g), z[...], 1, 0, HIGH)
    factor[...] = qv * scale
    hi, lo = split(qv)
    lhs = jnp.concatenate([hi, lo], 0)
    k = sketch.shape[0]
    group = 4

    def step(i, acc):
        copy(i).wait()
        for b in range(rows):
            hi, lo = split(wx[i * rows + b])
            o = dot(lhs, jnp.concatenate([hi, lo], 1))
            o = (o[r2:, :nt] + o[:r2, nt:] + o[r2:, nt:]) + o[:r2, :nt]
            hi, lo = split(o)
            at = pl.multiple_of((i * rows + b) * r2, r2)
            part[pl.ds(at, r2), :] = jnp.concatenate([hi, lo], 1)
        for b in range(0, rows, group):
            n = group * r2
            s = pl.ds(pl.multiple_of((i * rows + b) * r2, n), n)
            hi, lo = split(sketch[:, s])
            acc = acc + dot(jnp.concatenate([hi, lo], 0), part[s, :])
        return acc

    acc = jnp.zeros((2 * k, 2 * nt), F32)
    for i in range(chunks):
        acc = step(i, acc)
    total = (acc[k:, :nt] + acc[:k, nt:] + acc[k:, nt:]) + acc[:k, :nt]
    for i in range(zt.shape[0]):
        zt[i] = total


def third(grams, z, sketch, wa, scale, copies, r1):
    r2, ny = z.shape
    nt = wa.shape[2]
    k = sketch.shape[0]
    return pl.pallas_call(
        lambda *a: third_kernel(scale, *a),
        in_specs=[VMEM] * 6 + [HBM],
        out_specs=[VMEM] * 3,
        out_shape=[
            jax.ShapeDtypeStruct((r2, ny), F32),
            jax.ShapeDtypeStruct((r1 * r2, 2 * nt), BF16),
            jax.ShapeDtypeStruct((copies, k, nt), F32),
        ],
        scratch_shapes=[pltpu.VMEM((r1, ny, nt), F32), pltpu.SemaphoreType.DMA((2,))],
        compiler_params=room(BIG),
    )(*grams, z, sketch, wa)


def core_kernel(parts, part, z, gram, out):
    total = tree_sum([parts[i] for i in range(parts.shape[0])])
    z[...] = total
    gram[...] = dot(total, total, 1, 1, HIGH)
    k = total.shape[0]
    lhs = twice(total)
    group = lax.broadcasted_iota(jnp.int32, (8, 128), 1) // 32
    for i in range(part.shape[0] // 256):
        o = dot(lhs, part[i * 256 : (i + 1) * 256, :], 1, 1)
        o = o[k:] + o[:k]
        for j in range(2):
            v = [o[8 * g : 8 * g + 8, 128 * j : 128 * j + 128] for g in range(4)]
            for s in range(4):
                t = None
                for g in range(4):
                    shift = (g - s) * 32 % 128
                    u = pltpu.roll(v[g], shift, 1) if shift else v[g]
                    t = u if t is None else jnp.where(group == g, u, t)
                at = i * 4 + j * 2 + s // 2
                out[at, 8 * (s % 2) : 8 * (s % 2) + 8, :] = t


def core_terms(parts, part, r1):
    k, nt = parts.shape[1:]
    return pl.pallas_call(
        core_kernel,
        in_specs=[VMEM, VMEM],
        out_specs=[VMEM] * 3,
        out_shape=[
            jax.ShapeDtypeStruct((k, nt), F32),
            jax.ShapeDtypeStruct((k, k), F32),
            jax.ShapeDtypeStruct((r1, 16, 128), F32),
        ],
        compiler_params=room(MIDDLE),
    )(parts, part)


def inverse_kernel(scale, g0, g1, g2, g3, z, factor, inv):
    inv[...] = cholesky_inverse((g0[...] + g1[...]) + (g2[...] + g3[...]))
    factor[...] = dot(inv[...], z[...], 1, 0, HIGH) * scale


def last_factor(grams, z, scale):
    k, nt = z.shape
    return pl.pallas_call(
        lambda *a: inverse_kernel(scale, *a),
        in_specs=[VMEM] * 5,
        out_specs=[VMEM] * 2,
        out_shape=[jax.ShapeDtypeStruct((k, nt), F32), jax.ShapeDtypeStruct((k, k), F32)],
        compiler_params=room(MIDDLE),
        cost_estimate=pl.CostEstimate(flops=10**7, bytes_accessed=2 * 10**6, transcendentals=0),
    )(*grams, z)


def scale_kernel(core_id, inv, own, other, out, held):
    piece = own[...] + other[...]
    piece = jnp.where(core_id[0] == 0, piece[:8], piece[8:])
    x = jnp.concatenate([piece[:, 32 * g : 32 * g + 32] for g in range(4)], 0)
    held[...] = dot(x, inv[...], 0, 1, HIGH)
    row = jnp.concatenate([held[pl.ds(s, 8, stride=4), :] for s in range(4)], 1)
    for i in range(out.shape[0]):
        out[i] = row


def scaled(core_id, inv, own, other, copies):
    k = inv.shape[0]
    return pl.pallas_call(
        scale_kernel,
        in_specs=[SMEM] + [VMEM] * 3,
        out_specs=VMEM,
        out_shape=jax.ShapeDtypeStruct((copies, 8, 128), F32),
        scratch_shapes=[pltpu.VMEM((k, k), F32)],
        compiler_params=room(MIDDLE),
    )(core_id, inv, own, other)


def join_kernel(core_id, own, other, out):
    n, rows, _ = own.shape
    first = core_id[0] == 0
    half = rows * 128
    for b in range(0, n, 8):
        x = jnp.swapaxes(own[b : b + 8], 0, 1)
        y = jnp.swapaxes(other[b : b + 8], 0, 1)
        for r in range(rows):
            at = r * 128
            out[b : b + 8, at : at + 128] = jnp.where(first, x[r], y[r])
            out[b : b + 8, half + at : half + at + 128] = jnp.where(first, y[r], x[r])


def joined(core_id, own, other):
    n, rows, _ = own.shape
    return pl.pallas_call(
        join_kernel,
        in_specs=[SMEM, VMEM, VMEM],
        out_specs=VMEM,
        out_shape=jax.ShapeDtypeStruct((n, 2 * rows * 128), F32),
        compiler_params=room(MIDDLE),
    )(core_id, own, other)


def pair(x):
    return lax.ppermute(x, "c", [(0, 1), (1, 0)])


def exchange(x, axes):
    return lax.all_to_all(x, axes, 0, 0)


def of_four(x, axes):
    others = [lax.ppermute(x, axes, [(i, i ^ s) for i in range(4)]) for s in (3, 2, 1)]
    return [x] + others[::-1]


def spread(x, axes):
    n = math.prod(lax.axis_size(a) for a in axes)
    return exchange(jnp.broadcast_to(x, (n,) + x.shape), axes)


def both(x, axis):
    other = pair(x)
    first = lax.axis_index("c") == 0
    return jnp.where(
        first, jnp.concatenate([x, other], axis), jnp.concatenate([other, x], axis)
    )


def on_device(field, init_y, init_t, sketch_x, sketch_y, sketch_t):
    rows_x, rows_y, rows_t = field.shape
    r3 = init_t.shape[1]
    r1 = sketch_x.shape[1]
    scale_x = math.sqrt(rows_x * lax.axis_size(("y", "h")))
    scale_y = math.sqrt(rows_y * lax.axis_size("z"))
    scale_t = math.sqrt(rows_t * lax.axis_size(("l", "c")))
    core_id = lax.axis_index("c").astype(jnp.int32).reshape(1)

    w, zx = first(field, init_t.T, init_y.T, sketch_x.T, 8)
    zx = exchange(zx, ("z", "l")).sum(0)
    zx, gx = gram_of(8, zx[None], pair(zx)[None])
    sk_y = prepared_y(sketch_y.T, r3)
    u = project(zx, w, r3)
    gx, u = lax.optimization_barrier((exchange(gx, ("y", "h")), u))
    qx, factor_x, mine, other = second(core_id, gx, zx, sk_y, u, scale_x, r3)
    wx = contract_x(qx, field)
    zy = spread(mine + pair(other), ("y", "h", "l")).sum(0)
    zy, wx = lax.optimization_barrier((zy, wx))
    zy, gy = gram_of(1, both(zy, 0)[None])
    factor_y, part, zt = third(of_four(gy[0], "z"), zy, sketch_t.T, wx, scale_y, 32, r1)
    zt, gt, core = core_terms(exchange(zt, ("y", "h", "z")), part, r1)
    chips = ("y", "h", "z", "l")
    piece = exchange(core, chips).sum(0)
    factor_t, inv_t = last_factor(of_four(gt, ("l", "c")), zt, scale_t)
    piece, inv_t = lax.optimization_barrier((piece, inv_t))
    core = exchange(scaled(core_id, inv_t, piece, pair(piece), r1), chips)
    core = joined(core_id, core, pair(core))
    return factor_x.T, factor_y.T, factor_t.T, core


def solution(mesh):
    fine = Mesh(mesh.devices.reshape(4, 2, 4, 2, 2), ("y", "h", "z", "l", "c"))
    gx, gy, ta = ("y", "h"), "z", ("l", "c")
    in_specs = (P(gx, gy, ta), P(gy, None), P(ta, None), P(), P(), P())
    out_specs = (P(gx, None), P(gy, None), P(ta, None), P())
    return jax.shard_map(
        on_device, mesh=fine, in_specs=in_specs, out_specs=out_specs, check_vma=False
    )
```

```python
import math

import jax
import jax.numpy as jnp
from jax import lax
from jax.experimental import pallas as pl
from jax.experimental.pallas import tpu as pltpu
from jax.sharding import Mesh, PartitionSpec as P

HIGH = lax.Precision.HIGHEST
F32 = jnp.float32
BF16 = jnp.bfloat16
VMEM = pl.BlockSpec(memory_space=pltpu.VMEM)
HBM = pl.BlockSpec(memory_space=pltpu.HBM)
SMEM = pl.BlockSpec(memory_space=pltpu.SMEM)
MOST = 58 * 1024 * 1024
BIG = 49 * 1024 * 1024
AHEAD = 4
MIDDLE = 4 * 1024 * 1024


def room(size):
    return pltpu.CompilerParams(vmem_limit_bytes=size)


def split(x):
    hi = x.astype(BF16)
    return hi, (x - hi.astype(F32)).astype(BF16)


def twice(x):
    hi, lo = split(x)
    return jnp.concatenate([jnp.concatenate([hi, hi], 1), jnp.concatenate([lo, lo], 1)], 0)


def dot(a, b, da=1, db=0, precision=None):
    return lax.dot_general(
        a, b, (((da,), (db,)), ((), ())), precision=precision, preferred_element_type=F32
    )


def tree_sum(parts):
    parts = list(parts)
    while len(parts) > 1:
        even = [parts[i] + parts[i + 1] for i in range(0, len(parts) - 1, 2)]
        parts = even + parts[len(even) * 2 :]
    return parts[0]


def cholesky_inverse(g):
    n = g.shape[0]
    nb = n // 8
    lane = lax.broadcasted_iota(jnp.int32, (8, 128), 1)
    sub = lax.broadcasted_iota(jnp.int32, (8, 128), 0)
    blocks = []
    for k in range(nb):
        eye = (lane - n == sub + 8 * k).astype(F32)
        wide = jnp.concatenate([g[8 * k : 8 * k + 8, :], jnp.zeros((8, 128 - n), F32)], 1)
        blocks.append(jnp.where(lane < n, wide, eye))
    out = []
    for kb in range(nb):
        rows = blocks[kb]
        cols = [
            jnp.broadcast_to(rows[:, 8 * kb + j : 8 * kb + j + 1], (8, 128)) for j in range(8)
        ]
        done = rows
        for p in range(8):
            inv = 1.0 / cols[p][p : p + 1, :]
            at = sub == p
            done = jnp.where(at, rows * lax.rsqrt(cols[p]), done)
            pivot = rows[p : p + 1, :] * inv
            rows = jnp.where(at, pivot, rows - cols[p] * pivot)
            for j in range(p + 1, 8):
                c = cols[j][p : p + 1, :] * inv
                cols[j] = jnp.where(at, c, cols[j] - cols[p] * c)
        out.append(done)
        for m in range(kb + 1, nb):
            b = blocks[m]
            blocks[m] = b - tree_sum(
                [b[:, 8 * kb + j : 8 * kb + j + 1] * rows[j : j + 1, :] for j in range(8)]
            )
    return jnp.concatenate(out, 0)[:, n : 2 * n]


def fold(g):
    return jnp.concatenate([g[:32], g[32:]], 1)


def unfold(g):
    return jnp.concatenate([g[:, :64], g[:, 64:]], 0)


def first_kernel(
    field, init_t, init_y, sketch, w, z, held, pair_w, in_t, in_y, in_s, lhs, unfolded, sems, out_sems
):
    nx, ny, nt = held.shape
    r3, r2, k = init_t.shape[0], init_y.shape[0], sketch.shape[0]
    chunks = out_sems.shape[0]
    rows = nx // chunks

    def copy(i):
        s = pl.ds(i * rows, rows)
        return pltpu.make_async_copy(field.at[s], held.at[s], sems.at[i])

    def copy_out(i, part):
        s = pl.ds(pl.multiple_of(i * rows + part * nx, 16), rows)
        return pltpu.make_async_copy(
            pair_w.at[:, s, :], w.at[pl.ds(0, r3), s, :], out_sems.at[i, part]
        )

    small = [
        pltpu.make_async_copy(init_t, in_t, sems.at[chunks]),
        pltpu.make_async_copy(init_y, in_y, sems.at[chunks + 1]),
        pltpu.make_async_copy(sketch, in_s, sems.at[chunks + 2]),
    ]
    for c in small:
        c.start()
    for i in range(AHEAD):
        copy(i).start()
    small[0].wait()
    lhs[...] = twice(in_t[...])

    def chunk(i, _):
        copy(i).wait()

        @pl.when(i + AHEAD < chunks)
        def _():
            copy(i + AHEAD).start()

        groups = []
        for x8 in range(0, rows, 8):
            outs = []
            for x in range(8):
                hi, lo = split(held[i * rows + x8 + x])
                o = dot(lhs[...], jnp.concatenate([hi, lo], 1), 1, 1)
                outs.append(o[:r3] + o[r3:])
            groups.append(jnp.swapaxes(jnp.stack(outs, 0), 0, 1))
        hi, lo = split(jnp.concatenate(groups, 1))
        at = pl.multiple_of(i * rows, 16)
        pair_w[:, pl.ds(at, rows), :] = hi
        pair_w[:, pl.ds(pl.multiple_of(at + nx, 16), rows), :] = lo
        copy_out(i, 0).start()
        copy_out(i, 1).start()
        return 0

    lax.fori_loop(0, chunks, chunk, 0)
    small[1].wait()
    small[2].wait()
    hi, lo = split(in_y[...])
    left = jnp.concatenate([hi, lo], 0)
    for c8 in range(0, r3, 8):
        outs = []
        for c in range(c8, c8 + 8):
            o = dot(left, pair_w[c], 1, 1)
            outs.append((o[r2:, :nx] + o[:r2, nx:] + o[r2:, nx:]) + o[:r2, :nx])
        unfolded[:, c8 : c8 + 8, :] = jnp.swapaxes(jnp.stack(outs, 0), 0, 1)
    acc = None
    for a in range(0, r2, 8):
        hi, lo = split(unfolded[a : a + 8].reshape(8 * r3, nx))
        sh, sl = split(in_s[:, a * r3 : (a + 8) * r3])
        o = dot(jnp.concatenate([sh, sl], 0), jnp.concatenate([hi, lo], 1))
        acc = o if acc is None else acc + o
    total = (acc[k:, :nx] + acc[:k, nx:] + acc[k:, nx:]) + acc[:k, :nx]
    for i in range(z.shape[0]):
        z[i] = total
    for i in range(chunks):
        copy_out(i, 0).wait()
        copy_out(i, 1).wait()


def first(field, init_t, init_y, sketch, copies):
    nx, ny, nt = field.shape
    r3, r2, k = init_t.shape[0], init_y.shape[0], sketch.shape[0]
    return pl.pallas_call(
        first_kernel,
        in_specs=[HBM, HBM, HBM, HBM],
        out_specs=[HBM, VMEM],
        out_shape=[
            jax.ShapeDtypeStruct((4 * r3, 2 * nx, ny), BF16),
            jax.ShapeDtypeStruct((copies, k, nx), F32),
        ],
        scratch_shapes=[
            pltpu.VMEM((nx, ny, nt), F32),
            pltpu.VMEM((r3, 2 * nx, ny), BF16),
            pltpu.VMEM(init_t.shape, F32),
            pltpu.VMEM(init_y.shape, F32),
            pltpu.VMEM(sketch.shape, F32),
            pltpu.VMEM((2 * r3, 2 * nt), BF16),
            pltpu.VMEM((r2, r3, nx), F32),
            pltpu.SemaphoreType.DMA((11,)),
            pltpu.SemaphoreType.DMA((8, 2)),
        ],
        compiler_params=room(MOST),
        cost_estimate=pl.CostEstimate(
            flops=8 * nx * ny * nt * r3, bytes_accessed=nx * ny * nt * 4, transcendentals=0
        ),
    )(field, init_t, init_y, sketch)


def gram_kernel(*refs):
    *parts, z, gram = refs
    total = sum(tree_sum([p[i] for i in range(p.shape[0])]) for p in parts)
    z[...] = total
    g = fold(dot(total, total, 1, 1, HIGH))
    for i in range(gram.shape[0]):
        gram[i] = g


def gram_of(copies, *parts):
    k, n = parts[0].shape[1:]
    return pl.pallas_call(
        gram_kernel,
        in_specs=[VMEM] * len(parts),
        out_specs=[VMEM, VMEM],
        out_shape=[
            jax.ShapeDtypeStruct((k, n), F32),
            jax.ShapeDtypeStruct((copies, k * k // 128, 128), F32),
        ],
        compiler_params=room(MIDDLE),
    )(*parts)


def sketch_y_kernel(sketch, out, turned):
    k = sketch.shape[0]
    r3 = out.shape[0] // k
    r1 = sketch.shape[1] // r3
    for i in range(0, r1 * r3, 128):
        turned[i : i + 128, :] = sketch[:, i : i + 128].T
    for c in range(r3):
        hi, lo = split(turned[pl.ds(c, r1, stride=r3), :].T)
        out[c * k : (c + 1) * k, :] = jnp.concatenate([hi, lo, hi, lo], 1)


def prepared_y(sketch, r3):
    k, n = sketch.shape
    return pl.pallas_call(
        sketch_y_kernel,
        in_specs=[VMEM],
        out_specs=VMEM,
        out_shape=jax.ShapeDtypeStruct((r3 * k, 4 * n // r3), BF16),
        scratch_shapes=[pltpu.VMEM((n, k), F32)],
        compiler_params=room(MIDDLE),
        cost_estimate=pl.CostEstimate(flops=10**7, bytes_accessed=2 * 10**6, transcendentals=0),
    )(sketch)


def project_kernel(z, w, u, pair_w, sems):
    r3 = pair_w.shape[0]
    r1 = z.shape[0]
    each = r3 // sems.shape[0]

    def copy(i):
        s = pl.ds(i * each, each)
        return pltpu.make_async_copy(w.at[s], pair_w.at[s], sems.at[i])

    def start(i, _):
        copy(i).start()
        return 0

    lax.fori_loop(0, r3 // each, start, 0)
    lhs = twice(z[...])
    for c in range(r3):
        if c % each == 0:
            copy(c // each).wait()
        o = dot(lhs, pair_w[c])
        hi, lo = split(o[r1:] + o[:r1])
        u[c * r1 : (c + 1) * r1, :] = jnp.concatenate([hi, lo], 1)


def project(z, w, r3):
    r1, nx = z.shape
    ny = w.shape[2]
    return pl.pallas_call(
        project_kernel,
        in_specs=[VMEM, HBM],
        out_specs=VMEM,
        out_shape=jax.ShapeDtypeStruct((r3 * r1, 2 * ny), BF16),
        scratch_shapes=[
            pltpu.VMEM((r3, 2 * nx, ny), BF16),
            pltpu.SemaphoreType.DMA((2,)),
        ],
        compiler_params=room(BIG),
        cost_estimate=pl.CostEstimate(flops=10**9, bytes_accessed=6 * 10**6, transcendentals=0),
    )(z, w)


def second_kernel(scale, core_id, grams, z, sk, u, q, factor, mine, other):
    g = unfold(tree_sum([grams[i] for i in range(grams.shape[0])]))
    inv = cholesky_inverse(g)
    hi, lo = split(inv)
    mixed = dot(sk[...], jnp.concatenate([hi, hi, lo, lo], 0))
    half = mine.shape[0]
    k = 2 * half
    ny = mine.shape[1]
    r1 = z.shape[0]
    group = 4
    acc = None
    for c in range(0, mixed.shape[0] // k, group):
        left = jnp.concatenate([mixed[(c + i) * k : (c + i + 1) * k] for i in range(group)], 1)
        hi, lo = split(left)
        o = dot(jnp.concatenate([hi, lo], 0), u[c * r1 : (c + group) * r1, :])
        acc = o if acc is None else acc + o
    zy = (acc[k:, :ny] + acc[:k, ny:] + acc[k:, ny:]) + acc[:k, :ny]
    first = core_id[0] == 0
    mine[...] = jnp.where(first, zy[:half], zy[half:])
    other[...] = jnp.where(first, zy[half:], zy[:half])
    qv = dot(inv, z[...], 1, 0, HIGH)
    q[...] = qv
    factor[...] = qv * scale


def second(core_id, grams, z, sk, u, scale, r3):
    r1, nx = z.shape
    half = jax.ShapeDtypeStruct((sk.shape[0] // r3 // 2, u.shape[1] // 2), F32)
    return pl.pallas_call(
        lambda *a: second_kernel(scale, *a),
        in_specs=[SMEM] + [VMEM] * 4,
        out_specs=[VMEM] * 4,
        out_shape=[
            jax.ShapeDtypeStruct((r1, nx), F32),
            jax.ShapeDtypeStruct((r1, nx), F32),
            half,
            half,
        ],
        compiler_params=room(8 * 1024 * 1024),
    )(core_id, grams, z, sk, u)


def chunk_sizes(n):
    return [16] + [32] * ((n - 32) // 32) + [16]


def contract_x_kernel(q, field, wx, held, out, lhs, sems, out_sems):
    nx, ny, nt = held.shape
    r1 = q.shape[0]
    sizes = chunk_sizes(ny)
    chunks = len(sizes)

    def copy(i):
        s = pl.ds(sum(sizes[:i]), sizes[i])
        return pltpu.make_async_copy(field.at[:, s, :], held.at[:, s, :], sems.at[i])

    def copy_out(i):
        s = pl.ds(sum(sizes[:i]), sizes[i])
        return pltpu.make_async_copy(
            out.at[:, s, :], wx.at[pl.ds(0, r1), s, :], out_sems.at[i]
        )

    for i in range(AHEAD):
        copy(i).start()
    lhs[...] = twice(q[...])

    for i in range(chunks):
        copy(i).wait()
        if i + AHEAD < chunks:
            copy(i + AHEAD).start()
        for y8 in range(0, sizes[i], 8):
            at = sum(sizes[:i]) + y8
            f = jnp.swapaxes(held[:, pl.ds(at, 8), :], 0, 1)
            outs = []
            for y in range(0, 8, 2):
                h0, l0 = split(f[y])
                h1, l1 = split(f[y + 1])
                rhs = jnp.concatenate(
                    [jnp.concatenate([h0, h1], 1), jnp.concatenate([l0, l1], 1)], 0
                )
                o = dot(lhs[...], rhs)
                o = o[r1:] + o[:r1]
                outs += [o[:, :nt], o[:, nt:]]
            out[:, pl.ds(at, 8), :] = jnp.swapaxes(jnp.stack(outs, 0), 0, 1)
        copy_out(i).start()
    for i in range(chunks):
        copy_out(i).wait()


def contract_x(q, field):
    nx, ny, nt = field.shape
    r1 = q.shape[0]
    chunks = len(chunk_sizes(ny))
    return pl.pallas_call(
        contract_x_kernel,
        in_specs=[VMEM, HBM],
        out_specs=HBM,
        out_shape=jax.ShapeDtypeStruct((2 * r1, ny, nt), F32),
        scratch_shapes=[
            pltpu.VMEM((nx, ny, nt), F32),
            pltpu.VMEM((r1, ny, nt), F32),
            pltpu.VMEM((2 * r1, 2 * nx), BF16),
            pltpu.SemaphoreType.DMA((chunks,)),
            pltpu.SemaphoreType.DMA((chunks,)),
        ],
        compiler_params=room(BIG),
        cost_estimate=pl.CostEstimate(
            flops=8 * nx * ny * nt * r1, bytes_accessed=nx * ny * nt * 6, transcendentals=0
        ),
    )(q, field)


def third_kernel(scale, g0, g1, g2, g3, z, sketch, wa, factor, part, zt, wx, sems):
    r1, ny, nt = wx.shape
    r2 = z.shape[0]
    chunks = sems.shape[0]
    rows = r1 // chunks

    def copy(i):
        s = pl.ds(i * rows, rows)
        return pltpu.make_async_copy(wa.at[s], wx.at[s], sems.at[i])

    def start(i, _):
        copy(i).start()
        return 0

    lax.fori_loop(0, chunks, start, 0)
    g = unfold((g0[...] + g1[...]) + (g2[...] + g3[...]))
    qv = dot(cholesky_inverse(g), z[...], 1, 0, HIGH)
    factor[...] = qv * scale
    hi, lo = split(qv)
    lhs = jnp.concatenate([hi, lo], 0)
    k = sketch.shape[0]
    group = 4

    def step(i, acc):
        copy(i).wait()
        for b in range(rows):
            hi, lo = split(wx[i * rows + b])
            o = dot(lhs, jnp.concatenate([hi, lo], 1))
            o = (o[r2:, :nt] + o[:r2, nt:] + o[r2:, nt:]) + o[:r2, :nt]
            hi, lo = split(o)
            at = pl.multiple_of((i * rows + b) * r2, r2)
            part[pl.ds(at, r2), :] = jnp.concatenate([hi, lo], 1)
        for b in range(0, rows, group):
            n = group * r2
            s = pl.ds(pl.multiple_of((i * rows + b) * r2, n), n)
            hi, lo = split(sketch[:, s])
            acc = acc + dot(jnp.concatenate([hi, lo], 0), part[s, :])
        return acc

    acc = jnp.zeros((2 * k, 2 * nt), F32)
    for i in range(chunks):
        acc = step(i, acc)
    total = (acc[k:, :nt] + acc[:k, nt:] + acc[k:, nt:]) + acc[:k, :nt]
    for i in range(zt.shape[0]):
        zt[i] = total


def third(grams, z, sketch, wa, scale, copies, r1):
    r2, ny = z.shape
    nt = wa.shape[2]
    k = sketch.shape[0]
    return pl.pallas_call(
        lambda *a: third_kernel(scale, *a),
        in_specs=[VMEM] * 6 + [HBM],
        out_specs=[VMEM] * 3,
        out_shape=[
            jax.ShapeDtypeStruct((r2, ny), F32),
            jax.ShapeDtypeStruct((r1 * r2, 2 * nt), BF16),
            jax.ShapeDtypeStruct((copies, k, nt), F32),
        ],
        scratch_shapes=[pltpu.VMEM((r1, ny, nt), F32), pltpu.SemaphoreType.DMA((2,))],
        compiler_params=room(BIG),
    )(*grams, z, sketch, wa)


def core_kernel(parts, part, z, gram, out):
    total = tree_sum([parts[i] for i in range(parts.shape[0])])
    z[...] = total
    gram[...] = dot(total, total, 1, 1, HIGH)
    k = total.shape[0]
    lhs = twice(total)
    group = lax.broadcasted_iota(jnp.int32, (8, 128), 1) // 32
    for i in range(part.shape[0] // 256):
        o = dot(lhs, part[i * 256 : (i + 1) * 256, :], 1, 1)
        o = o[k:] + o[:k]
        for j in range(2):
            v = [o[8 * g : 8 * g + 8, 128 * j : 128 * j + 128] for g in range(4)]
            for s in range(4):
                t = None
                for g in range(4):
                    shift = (g - s) * 32 % 128
                    u = pltpu.roll(v[g], shift, 1) if shift else v[g]
                    t = u if t is None else jnp.where(group == g, u, t)
                at = i * 4 + j * 2 + s // 2
                out[at, 8 * (s % 2) : 8 * (s % 2) + 8, :] = t


def core_terms(parts, part, r1):
    k, nt = parts.shape[1:]
    return pl.pallas_call(
        core_kernel,
        in_specs=[VMEM, VMEM],
        out_specs=[VMEM] * 3,
        out_shape=[
            jax.ShapeDtypeStruct((k, nt), F32),
            jax.ShapeDtypeStruct((k, k), F32),
            jax.ShapeDtypeStruct((r1, 16, 128), F32),
        ],
        compiler_params=room(MIDDLE),
    )(parts, part)


def inverse_kernel(scale, g0, g1, g2, g3, z, factor, inv):
    inv[...] = cholesky_inverse((g0[...] + g1[...]) + (g2[...] + g3[...]))
    factor[...] = dot(inv[...], z[...], 1, 0, HIGH) * scale


def last_factor(grams, z, scale):
    k, nt = z.shape
    return pl.pallas_call(
        lambda *a: inverse_kernel(scale, *a),
        in_specs=[VMEM] * 5,
        out_specs=[VMEM] * 2,
        out_shape=[jax.ShapeDtypeStruct((k, nt), F32), jax.ShapeDtypeStruct((k, k), F32)],
        compiler_params=room(MIDDLE),
        cost_estimate=pl.CostEstimate(flops=10**7, bytes_accessed=2 * 10**6, transcendentals=0),
    )(*grams, z)


def scale_kernel(core_id, inv, own, other, out, held):
    piece = own[...] + other[...]
    piece = jnp.where(core_id[0] == 0, piece[:8], piece[8:])
    x = jnp.concatenate([piece[:, 32 * g : 32 * g + 32] for g in range(4)], 0)
    held[...] = dot(x, inv[...], 0, 1, HIGH)
    row = jnp.concatenate([held[pl.ds(s, 8, stride=4), :] for s in range(4)], 1)
    for i in range(out.shape[0]):
        out[i] = row


def scaled(core_id, inv, own, other, copies):
    k = inv.shape[0]
    return pl.pallas_call(
        scale_kernel,
        in_specs=[SMEM] + [VMEM] * 3,
        out_specs=VMEM,
        out_shape=jax.ShapeDtypeStruct((copies, 8, 128), F32),
        scratch_shapes=[pltpu.VMEM((k, k), F32)],
        compiler_params=room(MIDDLE),
    )(core_id, inv, own, other)


def join_kernel(core_id, own, other, out):
    n, rows, _ = own.shape
    first = core_id[0] == 0
    half = rows * 128
    for b in range(0, n, 8):
        x = jnp.swapaxes(own[b : b + 8], 0, 1)
        y = jnp.swapaxes(other[b : b + 8], 0, 1)
        for r in range(rows):
            at = r * 128
            out[b : b + 8, at : at + 128] = jnp.where(first, x[r], y[r])
            out[b : b + 8, half + at : half + at + 128] = jnp.where(first, y[r], x[r])


def joined(core_id, own, other):
    n, rows, _ = own.shape
    return pl.pallas_call(
        join_kernel,
        in_specs=[SMEM, VMEM, VMEM],
        out_specs=VMEM,
        out_shape=jax.ShapeDtypeStruct((n, 2 * rows * 128), F32),
        compiler_params=room(MIDDLE),
    )(core_id, own, other)


def pair(x):
    return lax.ppermute(x, "c", [(0, 1), (1, 0)])


def exchange(x, axes):
    return lax.all_to_all(x, axes, 0, 0)


def of_four(x, axes):
    others = [lax.ppermute(x, axes, [(i, i ^ s) for i in range(4)]) for s in (3, 2, 1)]
    return [x] + others[::-1]


def spread(x, axes):
    n = math.prod(lax.axis_size(a) for a in axes)
    return exchange(jnp.broadcast_to(x, (n,) + x.shape), axes)


def both(x, axis):
    other = pair(x)
    first = lax.axis_index("c") == 0
    return jnp.where(
        first, jnp.concatenate([x, other], axis), jnp.concatenate([other, x], axis)
    )


def on_device(field, init_y, init_t, sketch_x, sketch_y, sketch_t):
    rows_x, rows_y, rows_t = field.shape
    r3 = init_t.shape[1]
    r1 = sketch_x.shape[1]
    scale_x = math.sqrt(rows_x * lax.axis_size(("y", "h")))
    scale_y = math.sqrt(rows_y * lax.axis_size("z"))
    scale_t = math.sqrt(rows_t * lax.axis_size(("l", "c")))
    core_id = lax.axis_index("c").astype(jnp.int32).reshape(1)

    w, zx = first(field, init_t.T, init_y.T, sketch_x.T, 8)
    zx = exchange(zx, ("z", "l")).sum(0)
    zx, gx = gram_of(8, zx[None], pair(zx)[None])
    sk_y = prepared_y(sketch_y.T, r3)
    u = project(zx, w, r3)
    gx, u = lax.optimization_barrier((exchange(gx, ("y", "h")), u))
    qx, factor_x, mine, other = second(core_id, gx, zx, sk_y, u, scale_x, r3)
    wx = contract_x(qx, field)
    zy = spread(mine + pair(other), ("y", "h", "l")).sum(0)
    zy, wx = lax.optimization_barrier((zy, wx))
    zy, gy = gram_of(1, both(zy, 0)[None])
    factor_y, part, zt = third(of_four(gy[0], "z"), zy, sketch_t.T, wx, scale_y, 32, r1)
    zt, gt, core = core_terms(exchange(zt, ("y", "h", "z")), part, r1)
    chips = ("y", "h", "z", "l")
    piece = exchange(core, chips).sum(0)
    factor_t, inv_t = last_factor(of_four(gt, ("l", "c")), zt, scale_t)
    piece, inv_t = lax.optimization_barrier((piece, inv_t))
    core = exchange(scaled(core_id, inv_t, piece, pair(piece), r1), chips)
    core = joined(core_id, core, pair(core))
    return factor_x.T, factor_y.T, factor_t.T, core


def solution(mesh):
    fine = Mesh(mesh.devices.reshape(4, 2, 4, 2, 2), ("y", "h", "z", "l", "c"))
    gx, gy, ta = ("y", "h"), "z", ("l", "c")
    in_specs = (P(gx, gy, ta), P(gy, None), P(ta, None), P(), P(), P())
    out_specs = (P(gx, None), P(gy, None), P(ta, None), P())
    return jax.shard_map(
        on_device, mesh=fine, in_specs=in_specs, out_specs=out_specs, check_vma=False
    )
```
